128 devices in a mesh: rows: 32 (over z_hi, x, y), cols: 4 (over z_lo, core).
Axes of the slice: x: 4, y: 4, z: 4 (z_hi: 2, z_lo: 2; z = z_hi * 2 + z_lo), core: 2. Of those that a mesh axis runs over, the one named last changes fastest.
Arguments:
- gradient: bfloat16 [8192, 7168], P('rows', 'cols'), may hold values from -0.21484375 to 0.21484375
- stat_old: float32 [8192, 8192], P('cols', 'rows'), may hold values from -4 to 6, as said below
Outputs:
- stat_new: float32 [8192, 8192], P('cols', 'rows')
The draws below stay inside these ranges and needn't reach their ends.
Inputs may be any that keep to these rules, and one draw needn't show every extreme that they name: `stat_old`: symmetric.
All inputs are finite; a program needn't handle non-finite values.
Results may differ from the reference program's by a relative error of at most 0.0003.
Values may be sent and summed in bfloat16 or wider, within the bound.
No kernel may reach another device: no remote copies, remote signals or barrier semaphores. Data moves between devices by JAX's collectives and lax.ppermute only.
A program may use at most 128 MiB of HBM per device.

```python
import jax
import jax.numpy as jnp
from jax import lax

M = 8192
K = 7168


def draw_stat_old(key, part):
    key = jax.random.fold_in(key, 7)
    entries = jnp.clip(jax.random.normal(key, (M, M), jnp.float32), -4.0, 4.0)
    index_row = lax.broadcasted_iota(jnp.int32, (M, M), 0)
    index_col = lax.broadcasted_iota(jnp.int32, (M, M), 1)
    diagonal = jnp.where(index_row == index_col, 2.0, 0.0).astype(jnp.float32)
    return 0.5 * (entries + entries.T) + diagonal


def shard_levels(own_key, shape, split, smallest, top_value):
    gain, own = 1.0, jax.random.fold_in(own_key, 6)
    for axis_at, shards_of in split:
        heights = jnp.exp(jax.random.uniform(jax.random.fold_in(own, axis_at), (shards_of,), jnp.float32, smallest / len(split), top_value / len(split)))
        gain = gain * jnp.repeat(heights, shape[axis_at] // shards_of).reshape([-1 if axis == axis_at else 1 for axis in range(len(shape))])
    return gain


def noise(own_key, extent, scale, limit, shards=(), held_as=jnp.bfloat16):
    array = scale * jax.random.normal(own_key, extent, jnp.float32)
    if shards:
        array = array * shard_levels(own_key, extent, shards, -0.22, 0.18)
    return jnp.clip(array, -limit, limit).astype(held_as)


def setup_inputs(seed: int = 0) -> dict:
    seeds = jax.random.split(jax.random.key(seed), 3)
    return {
        "gradient": noise(seeds[0], (M, K), (K ** -0.375), 0.21484375, ((0, 32), (1, 4))),
        "stat_old": draw_stat_old(jax.random.fold_in(seeds[2], 71), 0),
    }


def reference(gradient, stat_old):
    wide = gradient.astype(jnp.float32)
    gram = lax.dot_general(wide, wide, (((1,), (1,)), ((), ())), precision=lax.Precision.HIGHEST, preferred_element_type=jnp.float32)
    return 0.9 * stat_old + 0.1 * gram
```

```python
import functools

import jax
import jax.numpy as jnp
import numpy as np
from jax import lax
from jax.experimental import pallas as pl
from jax.experimental.pallas import tpu as pltpu
from jax.sharding import PartitionSpec as P

AXES = ("rows", "cols")
SIZES = (2, 4, 4, 2, 2)
WIRE = jnp.float16
SCALE = 128.0

NEAR = (("s", "s"), ("r1", "s"), ("c3", "s"), ("r1", "c1"), ("r3", "c1"))
FAR = (("r2", "s"), ("c2", "s"), ("c3", "r2"), ("r3", "c2"), ("r2", "c2"))
OFFSET = {"s": (0, 0), "r1": (1, 0), "r2": (2, 0), "r3": (3, 0), "c1": (0, 1), "c2": (0, 2), "c3": (0, 3)}


def route(move):
    pairs = []
    for source in range(int(np.prod(SIZES))):
        place = [int(i) for i in np.unravel_index(source, SIZES)]
        pairs.append((source, int(np.ravel_multi_index(move(*place), SIZES))))
    return pairs


def send(value, move):
    return lax.ppermute(value, AXES, route(move))


def shift(dx, dy, swap=False):
    def move(zh, x, y, zl, core):
        if swap:
            zh, zl = zl, zh
        return zh, (x + dx) % 4, (y + dy) % 4, zl, core

    return move


def other_core(zh, x, y, zl, core):
    return zh, x, y, zl, 1 - core


def other_high(zh, x, y, zl, core):
    return 1 - zh, x, y, zl, core


def first_partner(zh, x, y, zl, core):
    return (zh, x, y, 1 - zl, core) if core == 0 else (1 - zh, x, y, 1 - zl, core)


def second_partner(zh, x, y, zl, core):
    return first_partner(zh, x, y, zl, 1 - core)[:4] + (core,)


def products(blocks, pairs, half):
    out = {}
    for right in dict.fromkeys(r for _, r in pairs):
        lefts = [l for l, r in pairs if r == right]
        rows = [
            lax.dynamic_slice_in_dim(blocks[l][kind], half * 128, 128, 0) for l in lefts for kind in (0, 1)
        ]
        full = lax.dot_general(
            jnp.concatenate(rows),
            jnp.concatenate(blocks[right]),
            (((1,), (1,)), ((), ())),
            preferred_element_type=jnp.float32,
        ).reshape(len(lefts), 2, 128, 2, 256)
        for i, l in enumerate(lefts):
            out[l, right] = full[i]
    return jnp.stack([out[p] for p in pairs])


def summed(blocks, pairs, straight, core):
    away = send(products(blocks, pairs, 1 - core), other_core)
    whole = (products(blocks, pairs, core) + away) * SCALE
    q0 = jnp.where(straight, whole[:, 0], whole[:, 1])
    q1 = jnp.where(straight, whole[:, 1], whole[:, 0])
    q1_early = jnp.where(core == 0, q1[:, :, 0], q1[:, :, 1])
    q1_late = jnp.where(core == 0, q1[:, :, 1], q1[:, :, 0])
    got = send(jnp.stack([q1_early, q0[:, :, 1]]).astype(WIRE), first_partner).astype(jnp.float32)
    late = send((q1_late + got[1]).astype(WIRE), second_partner).astype(jnp.float32)
    return (q0[:, :, 0] + got[0] + late) * (1.0 / SCALE)


def delivered(totals, pairs):
    by_rows, by_columns = {}, {}
    moves = {}
    for i, (left, right) in enumerate(pairs):
        to = OFFSET[right]
        rows = tuple((a - b) % 4 for a, b in zip(OFFSET[left], to))
        moves.setdefault((to, False), []).append((i, rows))
        twice = left == right or (left, right) in (("r2", "s"), ("c2", "s"), ("r2", "c2"))
        if not twice:
            to = OFFSET[left]
            rows = tuple((a - b) % 4 for a, b in zip(OFFSET[right], to))
            moves.setdefault((to, True), []).append((i, rows))
    for (to, swap), tiles in moves.items():
        picked = jnp.stack([totals[i] for i, _ in tiles])
        if to != (0, 0):
            picked = send(picked, shift(*to, swap))
        for n, (_, rows) in enumerate(tiles):
            if swap:
                by_columns[rows] = picked[n].T
            else:
                by_rows[rows] = picked[n]
    return by_rows, by_columns


def both_halves(by_rows, by_columns, core):
    mine = jnp.stack([*by_rows.values()])
    turned = jnp.stack([*by_columns.values()])
    far, far_turned = send(mine, other_core), send(turned, other_core)
    low = jnp.where(core == 0, mine, far)
    high = jnp.where(core == 0, far, mine)
    whole = jnp.concatenate([low, high], axis=1)
    low = jnp.where(core == 0, turned, far_turned)
    high = jnp.where(core == 0, far_turned, turned)
    whole_turned = jnp.concatenate([low, high], axis=2)
    tiles = {rows: whole[i] for i, rows in enumerate(by_rows)}
    tiles.update({rows: whole_turned[i] for i, rows in enumerate(by_columns)})
    return tiles


def update(index, tile, old, new):
    new[...] = 0.9 * old[...] + 0.1 * tile[0]


def body(gradient, stat_old):
    device, column = lax.axis_index("rows"), lax.axis_index("cols")
    zh, x, y = device // 16, (device // 4) % 4, device % 4
    zl, core = column // 2, column % 2
    straight = zh == zl
    keep = lax.dynamic_slice_in_dim(gradient, zh * 896, 896, 1)
    give = lax.dynamic_slice_in_dim(gradient, (1 - zh) * 896, 896, 1)
    moves = {"r1": (-1, 0), "r3": (1, 0), "c1": (0, -1), "c3": (0, 1)}
    own = {"s": keep}
    other = {"s": send(give, other_high)}
    for name, move in moves.items():
        own[name] = send(keep, shift(*move))
    for name, move in moves.items():
        other[name] = send(other["s"], shift(*move))
    own["r2"] = send(own["r1"], shift(*moves["r1"]))
    own["c2"] = send(own["c1"], shift(*moves["c1"]))
    other["r2"] = send(other["r3"], shift(*moves["r3"]))
    other["c2"] = send(other["c3"], shift(*moves["c3"]))
    blocks = {name: (own[name], other[name]) for name in own}
    tiles = {}
    for pairs in (NEAR, FAR):
        totals = summed(blocks, pairs, straight, core)
        tiles.update(both_halves(*delivered(totals, pairs), core))
    stacked = jnp.stack([tiles[dx, dy] for dx in range(4) for dy in range(4)])
    block = jnp.arange(8)
    index = ((block // 4 + 2 * core - x) % 4) * 4 + (block % 4 - y) % 4
    return pl.pallas_call(
        update,
        out_shape=jax.ShapeDtypeStruct((2048, 256), jnp.float32),
        grid_spec=pltpu.PrefetchScalarGridSpec(
            num_scalar_prefetch=1,
            grid=(8,),
            in_specs=[
                pl.BlockSpec((1, 256, 256), lambda i, index: (index[i], 0, 0)),
                pl.BlockSpec((256, 256), lambda i, index: (i, 0)),
            ],
            out_specs=pl.BlockSpec((256, 256), lambda i, index: (i, 0)),
        ),
    )(index.astype(jnp.int32), stacked, stat_old)


def solution(mesh):
    placed = (P("rows", "cols"), P("cols", "rows"))
    return jax.shard_map(
        body, mesh=mesh, in_specs=placed, out_specs=P("cols", "rows"), check_vma=False
    )
```

```python
import functools

import jax
import jax.numpy as jnp
import numpy as np
from jax import lax
from jax.experimental import pallas as pl
from jax.experimental.pallas import tpu as pltpu
from jax.sharding import PartitionSpec as P


AXES = ("rows", "cols")
SIZES = (2, 4, 4, 2, 2)
ALONG = {"s": (0, 0), "a1": (1, 0), "a2": (2, 0), "a3": (3, 0), "b1": (0, 1), "b2": (0, 2), "b3": (0, 3)}
SCALE = 128.0
NEAR = (
    ("a1", "s", ("right", "left"), False),
    ("a1", "a3", ("right",), False),
    ("a1", "b1", ("right", "left"), False),
    ("s", "s", ("right",), True),
)
FAR = (("a2", "b3", ("right", "left"), False), ("a2", "b2", ("right",), True))
VMEM = pl.BlockSpec(memory_space=pltpu.VMEM)
SMEM = pl.BlockSpec(memory_space=pltpu.SMEM)


def offset(name, core):
    dx, dy = ALONG[name]
    return (dx, dy) if core == 0 else (-dy % 4, dx)


def gap(name, start, core):
    return tuple((a - b) % 4 for a, b in zip(offset(name, core), offset(start, core)))


def send(value, move):
    pairs = []
    for source in range(int(np.prod(SIZES))):
        place = [int(i) for i in np.unravel_index(source, SIZES)]
        pairs.append((source, int(np.ravel_multi_index(move(*place), SIZES))))
    return lax.ppermute(value, AXES, pairs)


def to_place(name, swap=False):
    def move(zh, x, y, zl, core):
        dx, dy = offset(name, core)
        if swap:
            zh, zl = zl, zh
        return zh, (x + dx) % 4, (y + dy) % 4, zl, core

    return move


def other_core(zh, x, y, zl, core):
    return zh, x, y, zl, 1 - core


def other_high(zh, x, y, zl, core):
    return 1 - zh, x, y, zl, core


def first_partner(zh, x, y, zl, core):
    return (zh, x, y, 1 - zl, core) if core == 0 else (1 - zh, x, y, 1 - zl, core)


def second_partner(zh, x, y, zl, core):
    return first_partner(zh, x, y, zl, 1 - core)[:4] + (core,)


def after(value, *others):
    return lax.optimization_barrier((value, *others))[0]


def packed(value):
    return (value * SCALE).astype(jnp.float16)


def unpacked(value):
    return value.astype(jnp.float32) * (1.0 / SCALE)


def call(kernel, outs, *args, flops=0, scratch=()):
    size = sum(a.size * a.dtype.itemsize for a in args) + sum(int(np.prod(s)) * 4 for s in outs)
    return pl.pallas_call(
        kernel,
        out_shape=[jax.ShapeDtypeStruct(s, jnp.float32) for s in outs],
        in_specs=[SMEM] + [VMEM] * (len(args) - 1),
        out_specs=[VMEM] * len(outs),
        scratch_shapes=scratch,
        compiler_params=pltpu.CompilerParams(vmem_limit_bytes=48 * 2**20),
        cost_estimate=pl.CostEstimate(flops=flops, bytes_accessed=size, transcendentals=0),
    )(*args)


def spans(pairs):
    at, out = 0, []
    for *_, halved in pairs:
        out.append((at, 128 if halved else 256))
        at += out[-1][1]
    return out, at


def multiply(pairs, names, place, *refs):
    held = {}
    for name in names:
        parts = 4 if name[1:] == "2" else 2
        held[name], refs = refs[:parts], refs[parts:]
    out, line = refs
    core = place[3]
    straight = jnp.where(place[0] == place[2], 1, 0)
    mirror = pairs[0][1] if pairs[0][1][0] == "b" else "b1"

    @pl.when(core == 0)
    def _():
        for kind in (0, 1):
            line[kind] = held[mirror][kind][...]

    @pl.when(core == 1)
    def _():
        for kind in (0, 1):
            line[kind] = held["b3" if mirror == "b1" else "b1"][kind][...]

    def rows(name, kind):
        if name == mirror:
            return line[kind]
        if name[1:] == "2":
            return jnp.concatenate([held[name][2 * kind][...], held[name][2 * kind + 1][...]], axis=0)
        return held[name][kind][...]

    for (left, right, _, halved), (at, size) in zip(pairs, spans(pairs)[0], strict=True):
        for kind in (0, 1):
            if not halved:
                lhs = rows(left, kind)
            elif left == "a2":
                lhs = jnp.where(core == 0, held[left][2 * kind][...], held[left][2 * kind + 1][...])
            else:
                lhs = held[left][kind][pl.ds(pl.multiple_of(core * 128, 128), 128), :]
            ends = straight if kind == 0 else 1 - straight
            for col in (0, 1):
                slot = jnp.where(ends == 1, 1 if col else 2, jnp.where(core == col, 0, 3))
                out[slot, pl.ds(at, size)] = lax.dot_general(
                    lhs, rows(right, col), (((1,), (1,)), ((), ())), preferred_element_type=jnp.float32
                )


def finish(groups, place, stay, got, late, *outs):
    for parts, out in zip(groups, outs, strict=True):
        to = 0
        for at, size in parts:
            take = pl.ds(at, size)
            out[pl.ds(to, size)] = stay[2, take] + got[0, take] + late[take]
            to += size


def products(place, blocks, pairs):
    total = spans(pairs)[1]
    names = sorted({name for pair in pairs for name in pair[:2]} | {"b1", "b3"})
    return call(
        functools.partial(multiply, pairs, names),
        [(4, total, 256)],
        place,
        *[rows for name in names for rows in blocks[name]],
        flops=total * 4 * 2 * 256 * 1792,
        scratch=[pltpu.VMEM((2, 256, 1792), jnp.bfloat16)],
    )[0]


def summed(place, stay, leave, pairs):
    where = spans(pairs)[0]
    got = unpacked(send(leave, first_partner))
    late = unpacked(send(packed(stay[3] + got[1]), second_partner))
    messages = {}
    for (left, right, keepers, halved), span in zip(pairs, where, strict=True):
        for keeper in keepers:
            to, rows = (right, left) if keeper == "right" else (left, right)
            messages.setdefault((to, keeper == "left"), []).append((span, halved, [gap(rows, to, c) for c in (0, 1)]))
    groups = [[span for span, _, _ in parts] for parts in messages.values()]
    outs = call(
        functools.partial(finish, groups),
        [(sum(size for _, size in g), 256) for g in groups],
        place,
        stay,
        got,
        late,
    )
    delivered = []
    for ((to, turned), parts), out in zip(messages.items(), outs, strict=True):
        if to != "s":
            out = send(out, to_place(to, turned))
        layout = [(turned, halved, gaps) for _, halved, gaps in parts]
        delivered.append((layout, out, send(out, other_core)))
    return delivered


def update(layouts, place, old, *refs):
    new = refs[-1]
    core = place[3]
    for parts, mine, far in zip(layouts, refs[:-1:2], refs[1:-1:2], strict=True):
        for source, tiles in ((core, mine), (1 - core, far)):
            at = 0
            for turned, halved, gaps in parts:
                size = 128 if halved else 256
                dx = jnp.where(source == 0, gaps[0][0], gaps[1][0])
                dy = jnp.where(source == 0, gaps[0][1], gaps[1][1])
                x, y = (place[1] + dx) & 3, (place[4] + dy) & 3

                @pl.when((x >> 1) == core)
                def _():
                    tile = tiles[pl.ds(at, size)]
                    if turned:
                        tile = tile.T
                    to = ((x & 1) * 4 + y) * 256 + (source * 128 if halved else 0)
                    to = pl.ds(pl.multiple_of(to, 128), size)
                    new[to] = 0.9 * old[to] + 0.1 * tile

                at += size


def body(gradient, stat_old):
    device = lax.axis_index("rows").astype(jnp.int32)
    column = lax.axis_index("cols").astype(jnp.int32)
    zh, x, y = device >> 4, (device >> 2) & 3, device & 3
    zl, core = column >> 1, column & 1
    place = jnp.stack([zh, x, zl, core, y])

    def whole(rows):
        far = send(rows, other_core)
        first = jnp.where(core == 0, rows, far)
        return jnp.concatenate([first, jnp.where(core == 0, far, rows)], axis=1)

    keep = lax.dynamic_slice_in_dim(gradient, zh * 896, 896, 1)
    give = lax.dynamic_slice_in_dim(gradient, (1 - zh) * 896, 896, 1)
    own = {"s": whole(keep)}
    given = send(after(give, own["s"]), other_high)
    own["a1"], own["a3"] = send(own["s"], to_place("a3")), send(own["s"], to_place("a1"))
    other = {"s": whole(after(given, own["a1"], own["a3"]))}
    other["a1"], other["a3"] = send(other["s"], to_place("a3")), send(other["s"], to_place("a1"))
    for kind in (own, other):
        kind["b1"], kind["b3"] = send(kind["a1"], other_core), send(kind["a3"], other_core)
        upper, lower = send(kind["a1"][:128], to_place("a3")), send(kind["a3"][128:], to_place("a1"))
        kind["a2"] = upper, lower
        kind["b2"] = send(upper, other_core), send(lower, other_core)
    blocks = {name: (own[name], other[name]) for name in ("s", "a1", "a3", "b1", "b3")}
    blocks.update({name: own[name] + other[name] for name in ("a2", "b2")})
    near = products(place, blocks, NEAR)
    near_leave = packed(near[:2])
    far = products(after(place, near_leave), blocks, FAR)
    far_leave = packed(far[:2])
    delivered = summed(place, near, near_leave, NEAR) + summed(place, far, far_leave, FAR)
    (new,) = call(
        functools.partial(update, [layout for layout, _, _ in delivered]),
        [stat_old.shape],
        place,
        stat_old,
        *[tiles for _, mine, far in delivered for tiles in (mine, far)],
    )
    return new


def solution(mesh):
    placed = (P("rows", "cols"), P("cols", "rows"))
    return jax.shard_map(
        body, mesh=mesh, in_specs=placed, out_specs=P("cols", "rows"), check_vma=False
    )
```

```python
import functools

import jax
import jax.numpy as jnp
import numpy as np
from jax import lax
from jax.experimental import pallas as pl
from jax.experimental.pallas import tpu as pltpu
from jax.sharding import PartitionSpec as P


AXES = ("rows", "cols")
SIZES = (2, 4, 4, 2, 2)
ALONG = {"s": (0, 0), "a1": (1, 0), "a2": (2, 0), "a3": (3, 0), "b1": (0, 1), "b2": (0, 2), "b3": (0, 3)}
ROWS = 64.0 * 2.0 ** (np.arange(1024) * 0.6180339887 % 1 / 2)
COLUMNS = 2.0 ** (np.arange(256) * 0.7548776662 % 1 / 2)
FIRST = (
    ("a1", "s", ("right", "left"), False),
    ("a1", "a3", ("right",), False),
    ("s", "s", ("right",), True),
    ("a1", "b1", ("right", "left"), False),
)
SECOND = (("a2", "b3", ("right", "left"), False), ("a2", "b2", ("left",), True))
VMEM = pl.BlockSpec(memory_space=pltpu.VMEM)
SMEM = pl.BlockSpec(memory_space=pltpu.SMEM)


def offset(name, core):
    dx, dy = ALONG[name]
    return (dx, dy) if core == 0 else (-dy % 4, dx)


def gap(name, start, core):
    return tuple((a - b) % 4 for a, b in zip(offset(name, core), offset(start, core)))


def send(value, move):
    pairs = []
    for source in range(int(np.prod(SIZES))):
        place = [int(i) for i in np.unravel_index(source, SIZES)]
        pairs.append((source, int(np.ravel_multi_index(move(*place), SIZES))))
    return lax.ppermute(value, AXES, pairs)


def to_place(name, swap=False):
    def move(zh, x, y, zl, core):
        dx, dy = offset(name, core)
        if swap:
            zh, zl = zl, zh
        return zh, (x + dx) % 4, (y + dy) % 4, zl, core

    return move


def other_core(zh, x, y, zl, core):
    return zh, x, y, zl, 1 - core


def other_high(zh, x, y, zl, core):
    return 1 - zh, x, y, zl, core


def first_partner(zh, x, y, zl, core):
    return (zh, x, y, 1 - zl, core) if core == 0 else (1 - zh, x, y, 1 - zl, core)


def second_partner(zh, x, y, zl, core):
    return first_partner(zh, x, y, zl, 1 - core)[:4] + (core,)


def after(value, *others):
    return lax.optimization_barrier((value, *others))[0]


def packed(value):
    rows, columns = np.float32(ROWS[: value.shape[-2], None]), np.float32(COLUMNS)
    return (value * rows * columns).astype(jnp.float16)


def unpacked(value):
    rows, columns = np.float32(1 / ROWS[: value.shape[-2], None]), np.float32(1 / COLUMNS)
    return value.astype(jnp.float32) * rows * columns


def call(kernel, outs, place, *args, keep=True, cost=2**21):
    return pl.pallas_call(
        kernel,
        out_shape=[pltpu.VMEM(s, jnp.float32) if keep else jax.ShapeDtypeStruct(s, jnp.float32) for s in outs],
        in_specs=[SMEM] + [VMEM] * len(args),
        out_specs=[VMEM] * len(outs),
        compiler_params=pltpu.CompilerParams(vmem_limit_bytes=8 * 2**20),
        cost_estimate=pl.CostEstimate(flops=0, bytes_accessed=cost, transcendentals=0),
    )(place, *[pltpu.with_memory_space_constraint(a, pltpu.VMEM) for a in args])


def spans(pairs):
    at, out = 0, []
    for *_, halved in pairs:
        out.append((at, 128 if halved else 256))
        at += out[-1][1]
    return out, at


def multiply(pairs, names, place, *refs):
    held = {name: refs[2 * i : 2 * i + 2] for i, name in enumerate(names)}
    out = refs[-1]
    core = place[3]
    straight = jnp.where(place[0] == place[2], 1, 0)

    def pair(left, right, halved, at):
        for kind in (0, 1):
            ends = straight if kind == 0 else 1 - straight
            size = 128 if halved else 256
            lhs = held[left][kind][pl.ds(pl.multiple_of(core * 128, 128), 128), :] if halved else held[left][kind][...]
            for col in (0, 1):
                slot = jnp.where(ends == 1, 1 if col else 2, jnp.where(core == col, 0, 3))
                out[slot, pl.ds(at, size)] = lax.dot_general(
                    lhs, held[right][col][...], (((1,), (1,)), ((), ())), preferred_element_type=jnp.float32
                )

    for (left, right, _, halved), (at, _) in zip(pairs, spans(pairs)[0], strict=True):
        if right in ("b1", "b3"):
            pl.when(core == 0)(functools.partial(pair, left, right, halved, at))
            pl.when(core == 1)(functools.partial(pair, left, {"b1": "b3", "b3": "b1"}[right], halved, at))
        else:
            pair(left, right, halved, at)


def finish(groups, place, stay, got, late, *outs):
    for parts, out in zip(groups, outs, strict=True):
        to = 0
        for at, size in parts:
            take = pl.ds(at, size)
            out[pl.ds(to, size)] = stay[2, take] + got[0, take] + late[take]
            to += size


def products(place, blocks, pairs):
    names = {name for pair in pairs for name in pair[:2]}
    names = sorted(names | {"b1", "b3"})
    return call(
        functools.partial(multiply, pairs, names),
        [(4, spans(pairs)[1], 256)],
        place,
        *[rows for name in names for rows in blocks[name]],
        cost=2**24,
    )[0]


def delivered(place, stay, got, late, pairs):
    where = spans(pairs)[0]
    messages = {}
    for (left, right, keepers, halved), span in zip(pairs, where, strict=True):
        for keeper in keepers:
            to, rows = (right, left) if keeper == "right" else (left, right)
            messages.setdefault((to, keeper == "left"), []).append((span, halved, [gap(rows, to, c) for c in (0, 1)]))
    groups = [[span for span, _, _ in parts] for parts in messages.values()]
    outs = call(
        functools.partial(finish, groups),
        [(sum(size for _, size in g), 256) for g in groups],
        place,
        stay,
        got,
        late,
    )
    tiles = []
    for ((to, turned), parts), out in zip(messages.items(), outs, strict=True):
        if turned:
            out = packed(out)
        if to != "s":
            out = send(out, to_place(to, turned))
        far = send(out, other_core)
        if turned:
            out, far = unpacked(out), unpacked(far)
        tiles.append(([(turned, halved, gaps) for _, halved, gaps in parts], out, far))
    return tiles, outs


def update(layouts, place, old, *refs):
    new = refs[-1]
    core = place[3]
    for parts, mine, far in zip(layouts, refs[:-1:2], refs[1:-1:2], strict=True):
        for source, tiles in ((core, mine), (1 - core, far)):
            at = 0
            for turned, halved, gaps in parts:
                size = 128 if halved else 256
                dx = jnp.where(source == 0, gaps[0][0], gaps[1][0])
                dy = jnp.where(source == 0, gaps[0][1], gaps[1][1])
                x, y = (place[1] + dx) & 3, (place[4] + dy) & 3

                @pl.when((x >> 1) == core)
                def _():
                    tile = tiles[pl.ds(at, size)]
                    half = pl.multiple_of(source * 128, 128)
                    to = pl.multiple_of(((x & 1) * 4 + y) * 256, 256)
                    if turned:
                        tile = tile.T
                        to = pl.ds(to, 256), pl.ds(half, 128) if halved else slice(None)
                    else:
                        to = pl.ds(to + half, 128) if halved else pl.ds(to, 256), slice(None)
                    new[to] = 0.9 * old[to] + 0.1 * tile

                at += size


def body(gradient, stat_old):
    device = lax.axis_index("rows").astype(jnp.int32)
    column = lax.axis_index("cols").astype(jnp.int32)
    zh, x, y = device >> 4, (device >> 2) & 3, device & 3
    zl, core = column >> 1, column & 1
    place = jnp.stack([zh, x, zl, core, y])

    def whole(rows, *others):
        far = after(send(rows, other_core), *others)
        first = jnp.where(core == 0, rows, far)
        return jnp.concatenate([first, jnp.where(core == 0, far, rows)], axis=1)

    keep = lax.dynamic_slice_in_dim(gradient, zh * 896, 896, 1)
    give = lax.dynamic_slice_in_dim(gradient, (1 - zh) * 896, 896, 1)
    given = send(give, other_high)
    own = {"s": whole(keep)}
    own["a1"], own["a3"] = send(own["s"], to_place("a3")), send(own["s"], to_place("a1"))
    own["b1"], own["b3"] = send(own["a1"], other_core), send(own["a3"], other_core)
    other = {"s": whole(given, own["a1"], own["a3"])}
    other["a1"], other["a3"] = send(other["s"], to_place("a3")), send(other["s"], to_place("a1"))
    own["a2"] = send(after(own["a1"], other["a1"], own["b1"]), to_place("a3"))
    other["a2"] = send(after(other["a3"], own["b3"]), to_place("a1"))
    other["b1"], other["b3"] = send(other["a1"], other_core), send(other["a3"], other_core)
    blocks = {name: (own[name], other[name]) for name in own}

    stay1 = products(place, blocks, FIRST)
    leave1 = packed(stay1[:2])
    blocks["a2"] = after(blocks["a2"], leave1)
    blocks["b2"] = tuple(send(rows, other_core) for rows in blocks["a2"])
    stay2 = products(place, blocks, SECOND)
    leave2 = packed(stay2[:2])
    got1 = unpacked(after(send(leave1, first_partner), leave2))
    late1 = packed(stay1[3] + got1[1])
    got2 = unpacked(after(send(leave2, first_partner), late1))
    late2 = packed(stay2[3] + got2[1])
    late1 = unpacked(after(send(late1, second_partner), late2))
    tiles1, outs = delivered(place, stay1, got1, late1, FIRST)
    late2 = unpacked(after(send(late2, second_partner), *outs))
    tiles2, _ = delivered(place, stay2, got2, late2, SECOND)
    tiles = tiles1 + tiles2
    (new,) = call(
        functools.partial(update, [layout for layout, _, _ in tiles]),
        [stat_old.shape],
        place,
        stat_old,
        *[part for _, mine, far in tiles for part in (mine, far)],
        keep=False,
    )
    return new


def solution(mesh):
    placed = (P("rows", "cols"), P("cols", "rows"))
    return jax.shard_map(
        body, mesh=mesh, in_specs=placed, out_specs=P("cols", "rows"), check_vma=False
    )
```

```python
import functools

import jax
import jax.numpy as jnp
import numpy as np
from jax import lax
from jax.experimental import pallas as pl
from jax.experimental.pallas import tpu as pltpu
from jax.sharding import PartitionSpec as P


AXES = ("rows", "cols")
SIZES = (2, 4, 4, 2, 2)
ALONG = {"s": (0, 0), "a1": (1, 0), "a2": (2, 0), "a3": (3, 0), "b1": (0, 1), "b2": (0, 2), "b3": (0, 3)}
ROWS = 64.0 * 2.0 ** (np.arange(1024) * 0.6180339887 % 1 / 2)
COLUMNS = 2.0 ** (np.arange(256) * 0.7548776662 % 1 / 2)
NEAR = (
    ("a1", "s", ("right", "left"), False),
    ("a1", "a3", ("right",), False),
    ("a1", "b1", ("right", "left"), False),
)
SELF = (("s", "s", ("right",), True),)
FAR = (("b3", "a2", ("right", "left"), False),)
OPPOSITE = (("b2", "a2", ("right",), True),)
VMEM = pl.BlockSpec(memory_space=pltpu.VMEM)
SMEM = pl.BlockSpec(memory_space=pltpu.SMEM)


def offset(name, core):
    dx, dy = ALONG[name]
    return (dx, dy) if core == 0 else (-dy % 4, dx)


def gap(name, start, core):
    return tuple((a - b) % 4 for a, b in zip(offset(name, core), offset(start, core)))


def send(value, move):
    pairs = []
    for source in range(int(np.prod(SIZES))):
        place = [int(i) for i in np.unravel_index(source, SIZES)]
        pairs.append((source, int(np.ravel_multi_index(move(*place), SIZES))))
    return lax.ppermute(value, AXES, pairs)


def to_place(name, swap=False):
    def move(zh, x, y, zl, core):
        dx, dy = offset(name, core)
        if swap:
            zh, zl = zl, zh
        return zh, (x + dx) % 4, (y + dy) % 4, zl, core

    return move


def other_core(zh, x, y, zl, core):
    return zh, x, y, zl, 1 - core


def other_high(zh, x, y, zl, core):
    return 1 - zh, x, y, zl, core


def first_partner(zh, x, y, zl, core):
    return (zh, x, y, 1 - zl, core) if core == 0 else (1 - zh, x, y, 1 - zl, core)


def second_partner(zh, x, y, zl, core):
    return first_partner(zh, x, y, zl, 1 - core)[:4] + (core,)


def after(value, *others):
    return lax.optimization_barrier((value, *others))[0]


def packed(value):
    rows, columns = np.float32(ROWS[: value.shape[-2], None]), np.float32(COLUMNS)
    return (value * rows * columns).astype(jnp.float16)


def unpacked(value):
    rows, columns = np.float32(1 / ROWS[: value.shape[-2], None]), np.float32(1 / COLUMNS)
    return value.astype(jnp.float32) * rows * columns


def call(kernel, outs, place, *args, keep=True, cost=2**21):
    return pl.pallas_call(
        kernel,
        out_shape=[pltpu.VMEM(s, jnp.float32) if keep else jax.ShapeDtypeStruct(s, jnp.float32) for s in outs],
        in_specs=[SMEM] + [VMEM] * len(args),
        out_specs=[VMEM] * len(outs),
        compiler_params=pltpu.CompilerParams(vmem_limit_bytes=8 * 2**20),
        cost_estimate=pl.CostEstimate(flops=0, bytes_accessed=cost, transcendentals=0),
    )(place, *[pltpu.with_memory_space_constraint(a, pltpu.VMEM) for a in args])


def multiply(pairs, names, place, *refs):
    held = {name: refs[2 * i : 2 * i + 2] for i, name in enumerate(names)}
    out = refs[-1]
    core = place[3]
    straight = jnp.where(place[0] == place[2], 1, 0)

    def pair(left, right, halved, at):
        for kind in (0, 1):
            ends = straight if kind == 0 else 1 - straight
            lhs = held[left][kind]
            if halved and lhs.shape[0] == 256:
                lhs = lhs.at[pl.ds(pl.multiple_of(core * 128, 128), 128)]
            for col in (0, 1):
                slot = jnp.where(ends == 1, 1 if col else 2, jnp.where(core == col, 0, 3))
                out[slot, pl.ds(at, lhs.shape[0])] = lax.dot_general(
                    lhs[...], held[right][col][...], (((1,), (1,)), ((), ())), preferred_element_type=jnp.float32
                )

    at = 0
    for left, right, _, halved in pairs:
        if {left, right} & {"b1", "b3"}:
            mirror = {"b1": "b3", "b3": "b1"}
            pl.when(core == 0)(functools.partial(pair, left, right, halved, at))
            pl.when(core == 1)(functools.partial(pair, mirror.get(left, left), mirror.get(right, right), halved, at))
        else:
            pair(left, right, halved, at)
        at += 128 if halved else 256


def products(place, blocks, pairs, cost=0):
    names = {name for pair in pairs for name in pair[:2]}
    names = sorted(names | {"b1", "b3"} if names & {"b1", "b3"} else names)
    return call(
        functools.partial(multiply, pairs, names),
        [(4, sum(128 if halved else 256 for *_, halved in pairs), 256)],
        place,
        *[rows for name in names for rows in blocks[name]],
        cost=cost,
    )[0]


def finish(messages, place, *refs):
    outs = refs[-len(messages) :]
    for tiles, out in zip(messages, outs, strict=True):
        to = 0
        for size, terms in tiles:
            parts = [refs[i][pl.ds(at, size)] if slot is None else refs[i][slot, pl.ds(at, size)] for i, slot, at in terms]
            out[pl.ds(to, size)] = sum(parts[1:], parts[0])
            to += size


def delivered(place, arrays, tiles):
    messages = {}
    for (left, right, keepers, halved), terms in tiles:
        for keeper in keepers:
            to, rows = (right, left) if keeper == "right" else (left, right)
            part = (halved, [gap(rows, to, c) for c in (0, 1)], (128 if halved else 256, terms))
            messages.setdefault((to, keeper == "left"), []).append(part)
    sums = [[part[2] for part in parts] for parts in messages.values()]
    outs = call(functools.partial(finish, sums), [(sum(size for size, _ in m), 256) for m in sums], place, *arrays)
    kept = []
    for ((to, turned), parts), out in zip(messages.items(), outs, strict=True):
        if turned:
            out = packed(out)
        if to != "s":
            out = send(out, to_place(to, turned))
        kept.append(([(turned, halved, gaps) for halved, gaps, _ in parts], out))
    return kept, outs


def with_halves(kept):
    both = []
    for _, mine in kept:
        far = send(mine, other_core)
        both += [unpacked(part) if mine.dtype == jnp.float16 else part for part in (mine, far)]
    return [layout for layout, _ in kept], [pltpu.with_memory_space_constraint(part, pltpu.VMEM) for part in both]


def places(layouts, place, tiles):
    core = place[3]
    for parts, pair in zip(layouts, zip(tiles[::2], tiles[1::2]), strict=True):
        for source, ref in zip((core, 1 - core), pair):
            at = 0
            for turned, halved, gaps in parts:
                size = 128 if halved else 256
                dx = jnp.where(source == 0, gaps[0][0], gaps[1][0])
                dy = jnp.where(source == 0, gaps[0][1], gaps[1][1])
                x, y = (place[1] + dx) & 3, (place[4] + dy) & 3
                to = ((x & 1) * 4 + y) * 256 + (source * 128 if halved else 0)

                def tile(ref=ref, at=at, size=size, turned=turned):
                    return ref[pl.ds(at, size)].T if turned else ref[pl.ds(at, size)]

                yield (x >> 1) == core, pl.ds(pl.multiple_of(to, 128), size), tile
                at += size


def begin(layouts, place, old, *refs):
    new, out, sem = refs[-3:]
    new[...] = 0.9 * old[...]
    for ours, to, tile in places(layouts, place, refs[:-3]):

        @pl.when(ours)
        def _():
            new[to] += 0.1 * tile()

    copy = pltpu.make_async_copy(new, out, sem)
    copy.start()
    copy.wait()


def end(layouts, place, base, *refs):
    out, rows, sems = refs[-3:]
    copies = []
    for n, (ours, to, tile) in enumerate(places(layouts, place, refs[:-4])):
        size = to.size
        copy = pltpu.make_async_copy(rows.at[n, pl.ds(0, size)], out.at[to], sems.at[n])

        @pl.when(ours)
        def _():
            rows[n, pl.ds(0, size)] = base[to] + 0.1 * tile()
            copy.start()

        copies.append((ours, copy))
    for ours, copy in copies:
        pl.when(ours)(copy.wait)


def body(gradient, stat_old):
    device = lax.axis_index("rows").astype(jnp.int32)
    column = lax.axis_index("cols").astype(jnp.int32)
    zh, x, y = device >> 4, (device >> 2) & 3, device & 3
    zl, core = column >> 1, column & 1
    place = jnp.stack([zh, x, zl, core, y])
    gradient, place, zh, core = lax.optimization_barrier((gradient, place, zh, core))
    first_core = core == 0

    def whole(rows, *others):
        far = after(send(rows, other_core), *others)
        first = jnp.where(first_core, rows, far)
        return jnp.concatenate([first, jnp.where(first_core, far, rows)], axis=1)

    keep = lax.dynamic_slice_in_dim(gradient, zh * 896, 896, 1)
    give = lax.dynamic_slice_in_dim(gradient, (1 - zh) * 896, 896, 1)
    given = send(give, other_high)
    own = {"s": whole(keep)}
    own["a1"], own["a3"] = send(own["s"], to_place("a3")), send(own["s"], to_place("a1"))
    own["b1"], own["b3"] = send(own["a1"], other_core), send(own["a3"], other_core)
    other = {"s": whole(given, own["a1"], own["a3"])}
    other["a1"], other["a3"] = send(other["s"], to_place("a3")), send(other["s"], to_place("a1"))
    made0 = products(place, {"s": (own["s"], other["s"])}, SELF)
    got0 = send(packed(made0[:2]), first_partner)
    late0 = send(packed(made0[3] + unpacked(got0[1])), second_partner)
    other["a1"], other["a3"] = after((other["a1"], other["a3"]), late0)
    own["a2"] = send(after(own["a1"], other["a1"], own["b1"]), to_place("a3"))
    other["a2"] = send(after(other["a3"], own["b3"]), to_place("a1"))
    other["b1"], other["b3"] = send(other["a1"], other_core), send(other["a3"], other_core)
    blocks = {name: (own[name], other[name]) for name in own}

    made1 = products(place, blocks, NEAR, 2**24)
    leave1 = packed(made1[0]), packed(made1[1])
    got1 = send(leave1[1], first_partner)
    a2 = after(blocks["a2"], got1)
    b2 = tuple(send(jnp.where(first_core, rows[128:], rows[:128]), other_core) for rows in a2)
    pass1 = packed(made1[3] + unpacked(got1))
    late1 = send(pass1, second_partner)
    rest1 = send(after(leave1[0], pass1), first_partner)
    made2 = products(after(place, pass1), {**blocks, "a2": a2}, FAR, 2**23)
    made3 = products(place, {"a2": a2, "b2": after(b2, made2)}, OPPOSITE, 2**23)
    leave2 = packed(jnp.concatenate([made2[:2], made3[:2]], axis=1))
    got2 = send(leave2, first_partner)
    at = [256 * i for i in range(4)]
    tiles1, _ = delivered(
        place,
        [made1, unpacked(after(rest1, leave2)), unpacked(after(late1, leave2)), made0, unpacked(got0[0]), unpacked(late0)],
        [(pair, [(0, 2, at[i]), (1, None, at[i]), (2, None, at[i])]) for i, pair in enumerate(NEAR)]
        + [(SELF[0], [(3, 2, 0), (4, None, 0), (5, None, 0)])],
    )
    pass2 = packed(jnp.concatenate([made2[3], made3[3]]) + unpacked(got2[1]))
    late2 = send(pass2, second_partner)
    tiles2, _ = delivered(
        place,
        [made2, made3, unpacked(got2[0]), unpacked(after(late2, *(mine for _, mine in tiles1)))],
        [
            (FAR[0], [(0, 2, 0), (2, None, 0), (3, None, 0)]),
            (OPPOSITE[0], [(1, 2, 0), (2, None, 256), (3, None, 256)]),
        ],
    )
    anywhere = pl.BlockSpec(memory_space=pl.ANY)
    params = pltpu.CompilerParams(vmem_limit_bytes=8 * 2**20)
    cost = pl.CostEstimate(flops=0, bytes_accessed=2**21, transcendentals=0)
    layouts, tiles = with_halves(tiles1)
    base, new = pl.pallas_call(
        functools.partial(begin, layouts),
        out_shape=[pltpu.VMEM(stat_old.shape, jnp.float32), jax.ShapeDtypeStruct(stat_old.shape, jnp.float32)],
        in_specs=[SMEM] + [VMEM] * (1 + len(tiles)),
        out_specs=[VMEM, anywhere],
        scratch_shapes=[pltpu.SemaphoreType.DMA],
        compiler_params=params,
        cost_estimate=cost,
    )(place, pltpu.with_memory_space_constraint(stat_old, pltpu.VMEM), *tiles)
    layouts, tiles = with_halves([(layout, after(mine, base)) for layout, mine in tiles2])
    count = 2 * sum(len(layout) for layout in layouts)
    return pl.pallas_call(
        functools.partial(end, layouts),
        out_shape=jax.ShapeDtypeStruct(stat_old.shape, jnp.float32),
        in_specs=[SMEM] + [VMEM] * (1 + len(tiles)) + [anywhere],
        out_specs=anywhere,
        scratch_shapes=[pltpu.VMEM((count, 256, 256), jnp.float32), pltpu.SemaphoreType.DMA((count,))],
        input_output_aliases={2 + len(tiles): 0},
        compiler_params=params,
        cost_estimate=cost,
    )(place, pltpu.with_memory_space_constraint(base, pltpu.VMEM), *tiles, new)


def solution(mesh):
    placed = (P("rows", "cols"), P("cols", "rows"))
    return jax.shard_map(
        body, mesh=mesh, in_specs=placed, out_specs=P("cols", "rows"), check_vma=False
    )
```

```python
import functools

import jax
import jax.numpy as jnp
import numpy as np
from jax import lax
from jax.experimental import pallas as pl
from jax.experimental.pallas import tpu as pltpu
from jax.sharding import PartitionSpec as P


AXES = ("rows", "cols")
SIZES = (2, 4, 4, 2, 2)
ALONG = {"s": (0, 0), "a1": (1, 0), "a2": (2, 0), "a3": (3, 0), "b1": (0, 1), "b2": (0, 2), "b3": (0, 3)}
ROWS = 64.0 * 2.0 ** (np.arange(1024) * 0.6180339887 % 1 / 2)
COLUMNS = 2.0 ** (np.arange(256) * 0.7548776662 % 1 / 2)
NEAR = (
    ("a1", "s", ("right", "left"), False),
    ("a1", "a3", ("right",), False),
    ("a1", "b1", ("right", "left"), False),
)
SELF = (("s", "s", ("right",), True),)
FAR = (("b3", "a2", ("right", "left"), False),)
OPPOSITE = (("b2", "a2", ("right",), True),)
VMEM = pl.BlockSpec(memory_space=pltpu.VMEM)
SMEM = pl.BlockSpec(memory_space=pltpu.SMEM)


def offset(name, core):
    dx, dy = ALONG[name]
    return (dx, dy) if core == 0 else (-dy % 4, dx)


def gap(name, start, core):
    return tuple((a - b) % 4 for a, b in zip(offset(name, core), offset(start, core)))


def send(value, move):
    pairs = []
    for source in range(int(np.prod(SIZES))):
        place = [int(i) for i in np.unravel_index(source, SIZES)]
        pairs.append((source, int(np.ravel_multi_index(move(*place), SIZES))))
    return lax.ppermute(value, AXES, pairs)


def to_place(name, swap=False):
    def move(zh, x, y, zl, core):
        dx, dy = offset(name, core)
        if swap:
            zh, zl = zl, zh
        return zh, (x + dx) % 4, (y + dy) % 4, zl, core

    return move


def other_core(zh, x, y, zl, core):
    return zh, x, y, zl, 1 - core


def other_high(zh, x, y, zl, core):
    return 1 - zh, x, y, zl, core


def first_partner(zh, x, y, zl, core):
    return (zh, x, y, 1 - zl, core) if core == 0 else (1 - zh, x, y, 1 - zl, core)


def second_partner(zh, x, y, zl, core):
    return first_partner(zh, x, y, zl, 1 - core)[:4] + (core,)


def after(value, *others):
    return lax.optimization_barrier((value, *others))[0]


def packed(value):
    rows, columns = np.float32(ROWS[: value.shape[-2], None]), np.float32(COLUMNS)
    return (value * rows * columns).astype(jnp.float16)


def unpacked(value):
    rows, columns = np.float32(1 / ROWS[: value.shape[-2], None]), np.float32(1 / COLUMNS)
    return value.astype(jnp.float32) * rows * columns


def call(kernel, outs, place, *args, keep=True, cost=2**21):
    return pl.pallas_call(
        kernel,
        out_shape=[pltpu.VMEM(s, jnp.float32) if keep else jax.ShapeDtypeStruct(s, jnp.float32) for s in outs],
        in_specs=[SMEM] + [VMEM] * len(args),
        out_specs=[VMEM] * len(outs),
        compiler_params=pltpu.CompilerParams(vmem_limit_bytes=8 * 2**20),
        cost_estimate=pl.CostEstimate(flops=0, bytes_accessed=cost, transcendentals=0),
    )(place, *[pltpu.with_memory_space_constraint(a, pltpu.VMEM) for a in args])


def multiply(pairs, names, place, *refs):
    held = {name: refs[2 * i : 2 * i + 2] for i, name in enumerate(names)}
    out = refs[-1]
    core = place[3]
    straight = jnp.where(place[0] == place[2], 1, 0)

    def pair(left, right, halved, at):
        for kind in (0, 1):
            ends = straight if kind == 0 else 1 - straight
            lhs = held[left][kind]
            if halved and lhs.shape[0] == 256:
                lhs = lhs.at[pl.ds(pl.multiple_of(core * 128, 128), 128)]
            for col in (0, 1):
                slot = jnp.where(ends == 1, 1 if col else 2, jnp.where(core == col, 0, 3))
                out[slot, pl.ds(at, lhs.shape[0])] = lax.dot_general(
                    lhs[...], held[right][col][...], (((1,), (1,)), ((), ())), preferred_element_type=jnp.float32
                )

    at = 0
    for left, right, _, halved in pairs:
        if {left, right} & {"b1", "b3"}:
            mirror = {"b1": "b3", "b3": "b1"}
            pl.when(core == 0)(functools.partial(pair, left, right, halved, at))
            pl.when(core == 1)(functools.partial(pair, mirror.get(left, left), mirror.get(right, right), halved, at))
        else:
            pair(left, right, halved, at)
        at += 128 if halved else 256


def products(place, blocks, pairs, cost=0):
    names = {name for pair in pairs for name in pair[:2]}
    names = sorted(names | {"b1", "b3"} if names & {"b1", "b3"} else names)
    return call(
        functools.partial(multiply, pairs, names),
        [(4, sum(128 if halved else 256 for *_, halved in pairs), 256)],
        place,
        *[rows for name in names for rows in blocks[name]],
        cost=cost,
    )[0]


def finish(messages, place, *refs):
    outs = refs[-len(messages) :]
    for tiles, out in zip(messages, outs, strict=True):
        to = 0
        for size, terms in tiles:
            parts = [refs[i][pl.ds(at, size)] if slot is None else refs[i][slot, pl.ds(at, size)] for i, slot, at in terms]
            out[pl.ds(to, size)] = sum(parts[1:], parts[0])
            to += size


def delivered(place, arrays, tiles):
    messages = {}
    for (left, right, keepers, halved), terms in tiles:
        for keeper in keepers:
            to, rows = (right, left) if keeper == "right" else (left, right)
            part = (halved, [gap(rows, to, c) for c in (0, 1)], (128 if halved else 256, terms))
            messages.setdefault((to, keeper == "left"), []).append(part)
    sums = [[part[2] for part in parts] for parts in messages.values()]
    outs = call(functools.partial(finish, sums), [(sum(size for size, _ in m), 256) for m in sums], place, *arrays)
    kept = []
    for ((to, turned), parts), out in zip(messages.items(), outs, strict=True):
        if turned or to == "a2":
            out = packed(out)
        if to != "s":
            out = send(out, to_place(to, turned))
        kept.append(([(turned, halved, gaps) for halved, gaps, _ in parts], out))
    return kept, outs


def with_halves(kept):
    both = []
    for _, mine in kept:
        far = send(mine, other_core)
        both += [unpacked(part) if mine.dtype == jnp.float16 else part for part in (mine, far)]
    return [layout for layout, _ in kept], [pltpu.with_memory_space_constraint(part, pltpu.VMEM) for part in both]


def places(layouts, place, tiles):
    core = place[3]
    for parts, pair in zip(layouts, zip(tiles[::2], tiles[1::2]), strict=True):
        for source, ref in zip((core, 1 - core), pair):
            at = 0
            for turned, halved, gaps in parts:
                size = 128 if halved else 256
                dx = jnp.where(source == 0, gaps[0][0], gaps[1][0])
                dy = jnp.where(source == 0, gaps[0][1], gaps[1][1])
                x, y = (place[1] + dx) & 3, (place[4] + dy) & 3
                to = ((x & 1) * 4 + y) * 256 + (source * 128 if halved else 0)

                def tile(ref=ref, at=at, size=size, turned=turned):
                    return ref[pl.ds(at, size)].T if turned else ref[pl.ds(at, size)]

                yield (x >> 1) == core, pl.ds(pl.multiple_of(to, 128), size), tile
                at += size


def begin(layouts, place, old, *refs):
    new, out, sem = refs[-3:]
    new[...] = 0.9 * old[...]
    for ours, to, tile in places(layouts, place, refs[:-3]):

        @pl.when(ours)
        def _():
            new[to] += 0.1 * tile()

    copy = pltpu.make_async_copy(new, out, sem)
    copy.start()
    copy.wait()


def end(layouts, place, base, *refs):
    out, rows, sems = refs[-3:]
    copies = []
    for n, (ours, to, tile) in enumerate(places(layouts, place, refs[:-4])):
        size = to.size
        copy = pltpu.make_async_copy(rows.at[n, pl.ds(0, size)], out.at[to], sems.at[n])

        @pl.when(ours)
        def _():
            rows[n, pl.ds(0, size)] = base[to] + 0.1 * tile()
            copy.start()

        copies.append((ours, copy))
    for ours, copy in copies:
        pl.when(ours)(copy.wait)


def body(gradient, stat_old):
    device = lax.axis_index("rows").astype(jnp.int32)
    column = lax.axis_index("cols").astype(jnp.int32)
    zh, x, y = device >> 4, (device >> 2) & 3, device & 3
    zl, core = column >> 1, column & 1
    place = jnp.stack([zh, x, zl, core, y])
    gradient, place, zh, core = lax.optimization_barrier((gradient, place, zh, core))
    first_core = core == 0

    def whole(rows, *others):
        far = after(send(rows, other_core), *others)
        first = jnp.where(first_core, rows, far)
        return jnp.concatenate([first, jnp.where(first_core, far, rows)], axis=1)

    keep = lax.dynamic_slice_in_dim(gradient, zh * 896, 896, 1)
    give = lax.dynamic_slice_in_dim(gradient, (1 - zh) * 896, 896, 1)
    given = send(give, other_high)
    own = {"s": whole(keep)}
    own["a1"], own["a3"] = send(own["s"], to_place("a3")), send(own["s"], to_place("a1"))
    own["b1"], own["b3"] = send(own["a1"], other_core), send(own["a3"], other_core)
    other = {"s": whole(given, own["a1"], own["a3"])}
    other["a1"], other["a3"] = send(other["s"], to_place("a3")), send(other["s"], to_place("a1"))
    made0 = products(place, {"s": (own["s"], other["s"])}, SELF)
    got0 = send(packed(made0[:2]), first_partner)
    late0 = send(packed(made0[3] + unpacked(got0[1])), second_partner)
    other["a1"], other["a3"] = after((other["a1"], other["a3"]), late0)
    own["a2"] = send(after(own["a1"], other["a1"], own["b1"]), to_place("a3"))
    other["a2"] = send(after(other["a3"], own["b3"]), to_place("a1"))
    other["b1"], other["b3"] = send(other["a1"], other_core), send(other["a3"], other_core)
    blocks = {name: (own[name], other[name]) for name in own}

    made1 = products(place, blocks, NEAR, 2**24)
    leave1 = packed(made1[0]), packed(made1[1])
    got1 = send(leave1[1], first_partner)
    a2 = after(blocks["a2"], got1)
    b2 = tuple(send(jnp.where(first_core, rows[128:], rows[:128]), other_core) for rows in a2)
    pass1 = packed(made1[3] + unpacked(got1))
    late1 = send(pass1, second_partner)
    rest1 = send(after(leave1[0], pass1), first_partner)
    made2 = products(after(place, pass1), {**blocks, "a2": a2}, FAR, 2**23)
    made3 = products(place, {"a2": a2, "b2": after(b2, made2)}, OPPOSITE, 2**23)
    leave2 = packed(jnp.concatenate([made2[:2], made3[:2]], axis=1))
    got2 = send(leave2, first_partner)
    at = [256 * i for i in range(4)]
    tiles1, _ = delivered(
        place,
        [made1, unpacked(after(rest1, leave2)), unpacked(after(late1, leave2)), made0, unpacked(got0[0]), unpacked(late0)],
        [(pair, [(0, 2, at[i]), (1, None, at[i]), (2, None, at[i])]) for i, pair in enumerate(NEAR)]
        + [(SELF[0], [(3, 2, 0), (4, None, 0), (5, None, 0)])],
    )
    pass2 = packed(jnp.concatenate([made2[3], made3[3]]) + unpacked(got2[1]))
    late2 = send(pass2, second_partner)
    tiles2, _ = delivered(
        place,
        [made2, made3, unpacked(got2[0]), unpacked(after(late2, *(mine for _, mine in tiles1)))],
        [
            (FAR[0], [(0, 2, 0), (2, None, 0), (3, None, 0)]),
            (OPPOSITE[0], [(1, 2, 0), (2, None, 256), (3, None, 256)]),
        ],
    )
    anywhere = pl.BlockSpec(memory_space=pl.ANY)
    params = pltpu.CompilerParams(vmem_limit_bytes=8 * 2**20)
    cost = pl.CostEstimate(flops=0, bytes_accessed=2**21, transcendentals=0)
    layouts, tiles = with_halves(tiles1)
    base, new = pl.pallas_call(
        functools.partial(begin, layouts),
        out_shape=[pltpu.VMEM(stat_old.shape, jnp.float32), jax.ShapeDtypeStruct(stat_old.shape, jnp.float32)],
        in_specs=[SMEM] + [VMEM] * (1 + len(tiles)),
        out_specs=[VMEM, anywhere],
        scratch_shapes=[pltpu.SemaphoreType.DMA],
        compiler_params=params,
        cost_estimate=cost,
    )(place, pltpu.with_memory_space_constraint(stat_old, pltpu.VMEM), *tiles)
    layouts, tiles = with_halves([(layout, after(mine, base)) for layout, mine in tiles2])
    count = 2 * sum(len(layout) for layout in layouts)
    return pl.pallas_call(
        functools.partial(end, layouts),
        out_shape=jax.ShapeDtypeStruct(stat_old.shape, jnp.float32),
        in_specs=[SMEM] + [VMEM] * (1 + len(tiles)) + [anywhere],
        out_specs=anywhere,
        scratch_shapes=[pltpu.VMEM((count, 256, 256), jnp.float32), pltpu.SemaphoreType.DMA((count,))],
        input_output_aliases={2 + len(tiles): 0},
        compiler_params=params,
        cost_estimate=cost,
    )(place, pltpu.with_memory_space_constraint(base, pltpu.VMEM), *tiles, new)


def solution(mesh):
    placed = (P("rows", "cols"), P("cols", "rows"))
    return jax.shard_map(
        body, mesh=mesh, in_specs=placed, out_specs=P("cols", "rows"), check_vma=False
    )
```

```python
import functools

import jax
import jax.numpy as jnp
import numpy as np
from jax import lax
from jax.experimental import pallas as pl
from jax.experimental.pallas import tpu as pltpu
from jax.sharding import PartitionSpec as P


AXES = ("rows", "cols")
SIZES = (2, 4, 4, 2, 2)
ALONG = {"s": (0, 0), "a1": (1, 0), "a2": (2, 0), "a3": (3, 0), "b1": (0, 1), "b2": (0, 2), "b3": (0, 3)}
NEAR = (
    ("a1", "s", ("right", "left"), False),
    ("a1", "a3", ("right",), False),
    ("a1", "b1", ("right", "left"), False),
)
SELF = (("s", "s", ("right",), True),)
FAR = (("b3", "a2", ("right", "left"), False),)
OPPOSITE = (("b2", "a2", ("right",), True),)
VMEM = pl.BlockSpec(memory_space=pltpu.VMEM)
SMEM = pl.BlockSpec(memory_space=pltpu.SMEM)


def offset(name, core):
    dx, dy = ALONG[name]
    return (dx, dy) if core == 0 else (-dy % 4, dx)


def gap(name, start, core):
    return tuple((a - b) % 4 for a, b in zip(offset(name, core), offset(start, core)))


def send(value, move):
    pairs = []
    for source in range(int(np.prod(SIZES))):
        place = [int(i) for i in np.unravel_index(source, SIZES)]
        pairs.append((source, int(np.ravel_multi_index(move(*place), SIZES))))
    return lax.ppermute(value, AXES, pairs)


def to_place(name, swap=False):
    def move(zh, x, y, zl, core):
        dx, dy = offset(name, core)
        if swap:
            zh, zl = zl, zh
        return zh, (x + dx) % 4, (y + dy) % 4, zl, core

    return move


def other_core(zh, x, y, zl, core):
    return zh, x, y, zl, 1 - core


def other_high(zh, x, y, zl, core):
    return 1 - zh, x, y, zl, core


def first_partner(zh, x, y, zl, core):
    return (zh, x, y, 1 - zl, core) if core == 0 else (1 - zh, x, y, 1 - zl, core)


def second_partner(zh, x, y, zl, core):
    return first_partner(zh, x, y, zl, 1 - core)[:4] + (core,)


def after(value, *others):
    return lax.optimization_barrier((value, *others))[0]


def packed(value):
    return value


def unpacked(value):
    return value


def call(kernel, outs, place, *args, keep=True, cost=2**21):
    return pl.pallas_call(
        kernel,
        out_shape=[pltpu.VMEM(s, jnp.float32) if keep else jax.ShapeDtypeStruct(s, jnp.float32) for s in outs],
        in_specs=[SMEM] + [VMEM] * len(args),
        out_specs=[VMEM] * len(outs),
        compiler_params=pltpu.CompilerParams(vmem_limit_bytes=8 * 2**20),
        cost_estimate=pl.CostEstimate(flops=0, bytes_accessed=cost, transcendentals=0),
    )(place, *[pltpu.with_memory_space_constraint(a, pltpu.VMEM) for a in args])


def multiply(pairs, names, place, *refs):
    held = {name: refs[2 * i : 2 * i + 2] for i, name in enumerate(names)}
    out = refs[-1]
    core = place[3]
    straight = jnp.where(place[0] == place[2], 1, 0)

    def pair(left, right, halved, at):
        for kind in (0, 1):
            ends = straight if kind == 0 else 1 - straight
            lhs = held[left][kind]
            if halved and lhs.shape[0] == 256:
                lhs = lhs.at[pl.ds(pl.multiple_of(core * 128, 128), 128)]
            for col in (0, 1):
                slot = jnp.where(ends == 1, 1 if col else 2, jnp.where(core == col, 0, 3))
                out[slot, pl.ds(at, lhs.shape[0])] = lax.dot_general(
                    lhs[...], held[right][col][...], (((1,), (1,)), ((), ())), preferred_element_type=jnp.float32
                )

    at = 0
    for left, right, _, halved in pairs:
        if {left, right} & {"b1", "b3"}:
            mirror = {"b1": "b3", "b3": "b1"}
            pl.when(core == 0)(functools.partial(pair, left, right, halved, at))
            pl.when(core == 1)(functools.partial(pair, mirror.get(left, left), mirror.get(right, right), halved, at))
        else:
            pair(left, right, halved, at)
        at += 128 if halved else 256


def products(place, blocks, pairs, cost=0):
    names = {name for pair in pairs for name in pair[:2]}
    names = sorted(names | {"b1", "b3"} if names & {"b1", "b3"} else names)
    return call(
        functools.partial(multiply, pairs, names),
        [(4, sum(128 if halved else 256 for *_, halved in pairs), 256)],
        place,
        *[rows for name in names for rows in blocks[name]],
        cost=cost,
    )[0]


def finish(messages, place, *refs):
    outs = refs[-len(messages) :]
    for tiles, out in zip(messages, outs, strict=True):
        to = 0
        for size, terms in tiles:
            parts = [refs[i][pl.ds(at, size)] if slot is None else refs[i][slot, pl.ds(at, size)] for i, slot, at in terms]
            out[pl.ds(to, size)] = sum(parts[1:], parts[0])
            to += size


def delivered(place, arrays, tiles):
    messages = {}
    for (left, right, keepers, halved), terms in tiles:
        for keeper in keepers:
            to, rows = (right, left) if keeper == "right" else (left, right)
            part = (halved, [gap(rows, to, c) for c in (0, 1)], (128 if halved else 256, terms))
            messages.setdefault((to, keeper == "left"), []).append(part)
    sums = [[part[2] for part in parts] for parts in messages.values()]
    outs = call(functools.partial(finish, sums), [(sum(size for size, _ in m), 256) for m in sums], place, *arrays)
    kept = []
    for ((to, turned), parts), out in zip(messages.items(), outs, strict=True):
        if turned or to == "a2":
            out = packed(out)
        if to != "s":
            out = send(out, to_place(to, turned))
        kept.append(([(turned, halved, gaps) for halved, gaps, _ in parts], out))
    return kept, outs


def with_halves(kept):
    both = []
    for _, mine in kept:
        far = send(mine, other_core)
        both += [mine, far]
    return [layout for layout, _ in kept], [pltpu.with_memory_space_constraint(part, pltpu.VMEM) for part in both]


def places(layouts, place, tiles):
    core = place[3]
    for parts, pair in zip(layouts, zip(tiles[::2], tiles[1::2]), strict=True):
        for source, ref in zip((core, 1 - core), pair):
            at = 0
            for turned, halved, gaps in parts:
                size = 128 if halved else 256
                dx = jnp.where(source == 0, gaps[0][0], gaps[1][0])
                dy = jnp.where(source == 0, gaps[0][1], gaps[1][1])
                x, y = (place[1] + dx) & 3, (place[4] + dy) & 3
                to = ((x & 1) * 4 + y) * 256 + (source * 128 if halved else 0)

                def tile(ref=ref, at=at, size=size, turned=turned):
                    return ref[pl.ds(at, size)].T if turned else ref[pl.ds(at, size)]

                yield (x >> 1) == core, pl.ds(pl.multiple_of(to, 128), size), tile
                at += size


def begin(layouts, place, old, *refs):
    new, out, sem = refs[-3:]
    new[...] = 0.9 * old[...]
    for ours, to, tile in places(layouts, place, refs[:-3]):

        @pl.when(ours)
        def _():
            new[to] += 0.1 * tile()

    copy = pltpu.make_async_copy(new, out, sem)
    copy.start()
    copy.wait()


def end(layouts, place, base, *refs):
    out, rows, sems = refs[-3:]
    copies = []
    for n, (ours, to, tile) in enumerate(places(layouts, place, refs[:-4])):
        size = to.size
        copy = pltpu.make_async_copy(rows.at[n, pl.ds(0, size)], out.at[to], sems.at[n])

        @pl.when(ours)
        def _():
            rows[n, pl.ds(0, size)] = base[to] + 0.1 * tile()
            copy.start()

        copies.append((ours, copy))
    for ours, copy in copies:
        pl.when(ours)(copy.wait)


def body(gradient, stat_old):
    device = lax.axis_index("rows").astype(jnp.int32)
    column = lax.axis_index("cols").astype(jnp.int32)
    zh, x, y = device >> 4, (device >> 2) & 3, device & 3
    zl, core = column >> 1, column & 1
    place = jnp.stack([zh, x, zl, core, y])
    gradient, place, zh, core = lax.optimization_barrier((gradient, place, zh, core))
    first_core = core == 0

    def whole(rows, *others):
        far = after(send(rows, other_core), *others)
        first = jnp.where(first_core, rows, far)
        return jnp.concatenate([first, jnp.where(first_core, far, rows)], axis=1)

    keep = lax.dynamic_slice_in_dim(gradient, zh * 896, 896, 1)
    give = lax.dynamic_slice_in_dim(gradient, (1 - zh) * 896, 896, 1)
    given = send(give, other_high)
    own = {"s": whole(keep)}
    own["a1"], own["a3"] = send(own["s"], to_place("a3")), send(own["s"], to_place("a1"))
    own["b1"], own["b3"] = send(own["a1"], other_core), send(own["a3"], other_core)
    other = {"s": whole(given, own["a1"], own["a3"])}
    other["a1"], other["a3"] = send(other["s"], to_place("a3")), send(other["s"], to_place("a1"))
    made0 = products(place, {"s": (own["s"], other["s"])}, SELF)
    got0 = send(packed(made0[:2]), first_partner)
    late0 = send(packed(made0[3] + unpacked(got0[1])), second_partner)
    other["a1"], other["a3"] = after((other["a1"], other["a3"]), late0)
    own["a2"] = send(after(own["a1"], other["a1"], own["b1"]), to_place("a3"))
    other["a2"] = send(after(other["a3"], own["b3"]), to_place("a1"))
    other["b1"], other["b3"] = send(other["a1"], other_core), send(other["a3"], other_core)
    blocks = {name: (own[name], other[name]) for name in own}

    made1 = products(place, blocks, NEAR, 2**24)
    leave1 = packed(made1[0]), packed(made1[1])
    got1 = send(leave1[1], first_partner)
    a2 = after(blocks["a2"], got1)
    b2 = tuple(send(jnp.where(first_core, rows[128:], rows[:128]), other_core) for rows in a2)
    pass1 = packed(made1[3] + unpacked(got1))
    late1 = send(pass1, second_partner)
    rest1 = send(after(leave1[0], pass1), first_partner)
    made2 = products(after(place, pass1), {**blocks, "a2": a2}, FAR, 2**23)
    made3 = products(place, {"a2": a2, "b2": after(b2, made2)}, OPPOSITE, 2**23)
    leave2 = packed(jnp.concatenate([made2[:2], made3[:2]], axis=1))
    got2 = send(leave2, first_partner)
    at = [256 * i for i in range(4)]
    tiles1, _ = delivered(
        place,
        [made1, unpacked(after(rest1, leave2)), unpacked(after(late1, leave2)), made0, unpacked(got0[0]), unpacked(late0)],
        [(pair, [(0, 2, at[i]), (1, None, at[i]), (2, None, at[i])]) for i, pair in enumerate(NEAR)]
        + [(SELF[0], [(3, 2, 0), (4, None, 0), (5, None, 0)])],
    )
    pass2 = packed(jnp.concatenate([made2[3], made3[3]]) + unpacked(got2[1]))
    late2 = send(pass2, second_partner)
    tiles2, _ = delivered(
        place,
        [made2, made3, unpacked(got2[0]), unpacked(after(late2, *(mine for _, mine in tiles1)))],
        [
            (FAR[0], [(0, 2, 0), (2, None, 0), (3, None, 0)]),
            (OPPOSITE[0], [(1, 2, 0), (2, None, 256), (3, None, 256)]),
        ],
    )
    anywhere = pl.BlockSpec(memory_space=pl.ANY)
    params = pltpu.CompilerParams(vmem_limit_bytes=8 * 2**20)
    cost = pl.CostEstimate(flops=0, bytes_accessed=2**21, transcendentals=0)
    layouts, tiles = with_halves(tiles1)
    base, new = pl.pallas_call(
        functools.partial(begin, layouts),
        out_shape=[pltpu.VMEM(stat_old.shape, jnp.float32), jax.ShapeDtypeStruct(stat_old.shape, jnp.float32)],
        in_specs=[SMEM] + [VMEM] * (1 + len(tiles)),
        out_specs=[VMEM, anywhere],
        scratch_shapes=[pltpu.SemaphoreType.DMA],
        compiler_params=params,
        cost_estimate=cost,
    )(place, pltpu.with_memory_space_constraint(stat_old, pltpu.VMEM), *tiles)
    layouts, tiles = with_halves([(layout, after(mine, base)) for layout, mine in tiles2])
    count = 2 * sum(len(layout) for layout in layouts)
    return pl.pallas_call(
        functools.partial(end, layouts),
        out_shape=jax.ShapeDtypeStruct(stat_old.shape, jnp.float32),
        in_specs=[SMEM] + [VMEM] * (1 + len(tiles)) + [anywhere],
        out_specs=anywhere,
        scratch_shapes=[pltpu.VMEM((count, 256, 256), jnp.float32), pltpu.SemaphoreType.DMA((count,))],
        input_output_aliases={2 + len(tiles): 0},
        compiler_params=params,
        cost_estimate=cost,
    )(place, pltpu.with_memory_space_constraint(base, pltpu.VMEM), *tiles, new)


def solution(mesh):
    placed = (P("rows", "cols"), P("cols", "rows"))
    return jax.shard_map(
        body, mesh=mesh, in_specs=placed, out_specs=P("cols", "rows"), check_vma=False
    )
```

```python
import functools

import jax
import jax.numpy as jnp
import numpy as np
from jax import lax
from jax.experimental import pallas as pl
from jax.experimental.pallas import tpu as pltpu
from jax.sharding import PartitionSpec as P


AXES = ("rows", "cols")
SIZES = (2, 4, 4, 2, 2)
ALONG = {"s": (0, 0), "a1": (1, 0), "a2": (2, 0), "a3": (3, 0), "b1": (0, 1), "b2": (0, 2), "b3": (0, 3)}
ROWS = 64.0 * 2.0 ** (np.arange(1024) * 0.6180339887 % 1 / 2)
COLUMNS = 2.0 ** (np.arange(256) * 0.7548776662 % 1 / 2)
NEAR = (
    ("a1", "s", ("right", "left"), False),
    ("a1", "a3", ("right",), False),
    ("a1", "b1", ("right", "left"), False),
)
SELF = (("s", "s", ("right",), True),)
FAR = (("b3", "a2", ("right", "left"), False),)
OPPOSITE = (("b2", "a2", ("right",), True),)
VMEM = pl.BlockSpec(memory_space=pltpu.VMEM)
SMEM = pl.BlockSpec(memory_space=pltpu.SMEM)


def offset(name, core):
    dx, dy = ALONG[name]
    return (dx, dy) if core == 0 else (-dy % 4, dx)


def gap(name, start, core):
    return tuple((a - b) % 4 for a, b in zip(offset(name, core), offset(start, core)))


def send(value, move):
    pairs = []
    for source in range(int(np.prod(SIZES))):
        place = [int(i) for i in np.unravel_index(source, SIZES)]
        pairs.append((source, int(np.ravel_multi_index(move(*place), SIZES))))
    return lax.ppermute(value, AXES, pairs)


def to_place(name, swap=False):
    def move(zh, x, y, zl, core):
        dx, dy = offset(name, core)
        if swap:
            zh, zl = zl, zh
        return zh, (x + dx) % 4, (y + dy) % 4, zl, core

    return move


def other_core(zh, x, y, zl, core):
    return zh, x, y, zl, 1 - core


def other_high(zh, x, y, zl, core):
    return 1 - zh, x, y, zl, core


def first_partner(zh, x, y, zl, core):
    return (zh, x, y, 1 - zl, core) if core == 0 else (1 - zh, x, y, 1 - zl, core)


def second_partner(zh, x, y, zl, core):
    return first_partner(zh, x, y, zl, 1 - core)[:4] + (core,)


def after(value, *others):
    return lax.optimization_barrier((value, *others))[0]


def packed(value):
    rows, columns = np.float32(ROWS[: value.shape[-2], None]), np.float32(COLUMNS)
    return (value * rows * columns).astype(jnp.float16)


def unpacked(value):
    rows, columns = np.float32(1 / ROWS[: value.shape[-2], None]), np.float32(1 / COLUMNS)
    return value.astype(jnp.float32) * rows * columns


def call(kernel, outs, place, *args, keep=True, cost=2**21):
    return pl.pallas_call(
        kernel,
        out_shape=[pltpu.VMEM(s, jnp.float32) if keep else jax.ShapeDtypeStruct(s, jnp.float32) for s in outs],
        in_specs=[SMEM] + [VMEM] * len(args),
        out_specs=[VMEM] * len(outs),
        compiler_params=pltpu.CompilerParams(vmem_limit_bytes=8 * 2**20),
        cost_estimate=pl.CostEstimate(flops=0, bytes_accessed=cost, transcendentals=0),
    )(place, *[pltpu.with_memory_space_constraint(a, pltpu.VMEM) for a in args])


def multiply(pairs, names, place, *refs):
    held = {name: refs[2 * i : 2 * i + 2] for i, name in enumerate(names)}
    out = refs[-1]
    core = place[3]
    straight = jnp.where(place[0] == place[2], 1, 0)

    def pair(left, right, halved, at):
        for kind in (0, 1):
            ends = straight if kind == 0 else 1 - straight
            lhs = held[left][kind]
            if halved and lhs.shape[0] == 256:
                lhs = lhs.at[pl.ds(pl.multiple_of(core * 128, 128), 128)]
            for col in (0, 1):
                slot = jnp.where(ends == 1, 1 if col else 2, jnp.where(core == col, 0, 3))
                out[slot, pl.ds(at, lhs.shape[0])] = lax.dot_general(
                    lhs[...], held[right][col][...], (((1,), (1,)), ((), ())), preferred_element_type=jnp.float32
                )

    at = 0
    for left, right, _, halved in pairs:
        if {left, right} & {"b1", "b3"}:
            mirror = {"b1": "b3", "b3": "b1"}
            pl.when(core == 0)(functools.partial(pair, left, right, halved, at))
            pl.when(core == 1)(functools.partial(pair, mirror.get(left, left), mirror.get(right, right), halved, at))
        else:
            pair(left, right, halved, at)
        at += 128 if halved else 256


def products(place, blocks, pairs, cost=0):
    names = {name for pair in pairs for name in pair[:2]}
    names = sorted(names | {"b1", "b3"} if names & {"b1", "b3"} else names)
    return call(
        functools.partial(multiply, pairs, names),
        [(4, sum(128 if halved else 256 for *_, halved in pairs), 256)],
        place,
        *[rows for name in names for rows in blocks[name]],
        cost=cost,
    )[0]


def finish(messages, place, *refs):
    outs = refs[-len(messages) :]
    for tiles, out in zip(messages, outs, strict=True):
        to = 0
        for size, terms in tiles:
            parts = [refs[i][pl.ds(at, size)] if slot is None else refs[i][slot, pl.ds(at, size)] for i, slot, at in terms]
            out[pl.ds(to, size)] = sum(parts[1:], parts[0])
            to += size


def delivered(place, arrays, tiles):
    messages = {}
    for (left, right, keepers, halved), terms in tiles:
        for keeper in keepers:
            to, rows = (right, left) if keeper == "right" else (left, right)
            part = (halved, [gap(rows, to, c) for c in (0, 1)], (128 if halved else 256, terms))
            messages.setdefault((to, keeper == "left"), []).append(part)
    sums = [[part[2] for part in parts] for parts in messages.values()]
    outs = call(functools.partial(finish, sums), [(sum(size for size, _ in m), 256) for m in sums], place, *arrays)
    kept = []
    for ((to, turned), parts), out in zip(messages.items(), outs, strict=True):
        if turned or to == "a2":
            out = packed(out)
        if to != "s":
            out = send(out, to_place(to, turned))
        kept.append(([(turned, halved, gaps) for halved, gaps, _ in parts], out))
    return kept, outs


def with_halves(kept):
    both = []
    for _, mine in kept:
        far = send(mine, other_core)
        both += [unpacked(part) if mine.dtype == jnp.float16 else part for part in (mine, far)]
    return [layout for layout, _ in kept], [pltpu.with_memory_space_constraint(part, pltpu.VMEM) for part in both]


def places(layouts, place, tiles):
    core = place[3]
    for parts, pair in zip(layouts, zip(tiles[::2], tiles[1::2]), strict=True):
        for source, ref in zip((core, 1 - core), pair):
            at = 0
            for turned, halved, gaps in parts:
                size = 128 if halved else 256
                dx = jnp.where(source == 0, gaps[0][0], gaps[1][0])
                dy = jnp.where(source == 0, gaps[0][1], gaps[1][1])
                x, y = (place[1] + dx) & 3, (place[4] + dy) & 3
                to = ((x & 1) * 4 + y) * 256 + (source * 128 if halved else 0)

                def tile(ref=ref, at=at, size=size, turned=turned):
                    return ref[pl.ds(at, size)].T if turned else ref[pl.ds(at, size)]

                yield (x >> 1) == core, pl.ds(pl.multiple_of(to, 128), size), tile
                at += size


def begin(layouts, place, old, *refs):
    new, out, sem = refs[-3:]
    new[...] = 0.9 * old[...]
    for ours, to, tile in places(layouts, place, refs[:-3]):

        @pl.when(ours)
        def _():
            new[to] += 0.1 * tile()

    copy = pltpu.make_async_copy(new, out, sem)
    copy.start()
    copy.wait()


def end(layouts, place, base, *refs):
    out, rows, sems = refs[-3:]
    copies = []
    for n, (ours, to, tile) in enumerate(places(layouts, place, refs[:-4])):
        size = to.size
        copy = pltpu.make_async_copy(rows.at[n, pl.ds(0, size)], out.at[to], sems.at[n])

        @pl.when(ours)
        def _():
            rows[n, pl.ds(0, size)] = base[to] + 0.1 * tile()
            copy.start()

        copies.append((ours, copy))
    for ours, copy in copies:
        pl.when(ours)(copy.wait)


def body(gradient, stat_old):
    device = lax.axis_index("rows").astype(jnp.int32)
    column = lax.axis_index("cols").astype(jnp.int32)
    zh, x, y = device >> 4, (device >> 2) & 3, device & 3
    zl, core = column >> 1, column & 1
    place = jnp.stack([zh, x, zl, core, y])
    gradient, place, zh, core = lax.optimization_barrier((gradient, place, zh, core))
    first_core = core == 0

    def whole(rows, *others):
        far = after(send(rows, other_core), *others)
        first = jnp.where(first_core, rows, far)
        return jnp.concatenate([first, jnp.where(first_core, far, rows)], axis=1)

    keep = lax.dynamic_slice_in_dim(gradient, zh * 896, 896, 1)
    give = lax.dynamic_slice_in_dim(gradient, (1 - zh) * 896, 896, 1)
    given = send(give, other_high)
    own = {"s": whole(keep)}
    own["a1"], own["a3"] = send(own["s"], to_place("a3")), send(own["s"], to_place("a1"))
    own["b1"], own["b3"] = send(own["a1"], other_core), send(own["a3"], other_core)
    other = {"s": whole(given, own["a1"], own["a3"])}
    other["a1"], other["a3"] = send(other["s"], to_place("a3")), send(other["s"], to_place("a1"))
    made0 = products(place, {"s": (own["s"], other["s"])}, SELF)
    got0 = send(packed(made0[:2]), first_partner)
    late0 = send(packed(made0[3] + unpacked(got0[1])), second_partner)
    other["a1"], other["a3"] = after((other["a1"], other["a3"]), late0)
    own["a2"] = send(after(own["a1"], late0, own["b1"]), to_place("a3"))
    other["a2"] = send(after(other["a3"], own["b3"]), to_place("a1"))
    other["b1"], other["b3"] = send(other["a1"], other_core), send(other["a3"], other_core)
    blocks = {name: (own[name], other[name]) for name in own}

    made1 = products(place, blocks, NEAR, 2**24)
    leave1 = packed(made1[0]), packed(made1[1])
    got1 = send(leave1[1], first_partner)
    a2 = after(blocks["a2"], got1)
    b2 = tuple(send(jnp.where(first_core, rows[128:], rows[:128]), other_core) for rows in a2)
    pass1 = packed(made1[3] + unpacked(got1))
    late1 = send(pass1, second_partner)
    rest1 = send(after(leave1[0], pass1), first_partner)
    made2 = products(after(place, pass1), {**blocks, "a2": a2}, FAR, 2**23)
    made3 = products(place, {"a2": a2, "b2": after(b2, made2)}, OPPOSITE, 2**23)
    leave2 = packed(jnp.concatenate([made2[:2], made3[:2]], axis=1))
    got2 = send(leave2, first_partner)
    at = [256 * i for i in range(4)]
    tiles1, _ = delivered(
        place,
        [made1, unpacked(after(rest1, leave2)), unpacked(after(late1, leave2)), made0, unpacked(got0[0]), unpacked(late0)],
        [(pair, [(0, 2, at[i]), (1, None, at[i]), (2, None, at[i])]) for i, pair in enumerate(NEAR)]
        + [(SELF[0], [(3, 2, 0), (4, None, 0), (5, None, 0)])],
    )
    pass2 = packed(jnp.concatenate([made2[3], made3[3]]) + unpacked(got2[1]))
    late2 = send(pass2, second_partner)
    tiles2, _ = delivered(
        place,
        [made2, made3, unpacked(got2[0]), unpacked(after(late2, *(mine for _, mine in tiles1)))],
        [
            (FAR[0], [(0, 2, 0), (2, None, 0), (3, None, 0)]),
            (OPPOSITE[0], [(1, 2, 0), (2, None, 256), (3, None, 256)]),
        ],
    )
    anywhere = pl.BlockSpec(memory_space=pl.ANY)
    params = pltpu.CompilerParams(vmem_limit_bytes=8 * 2**20)
    cost = pl.CostEstimate(flops=0, bytes_accessed=2**21, transcendentals=0)
    received = [mine for _, mine in tiles1]
    layouts, tiles = with_halves([(layout, after(mine, *received)) for layout, mine in tiles1])
    base, new = pl.pallas_call(
        functools.partial(begin, layouts),
        out_shape=[pltpu.VMEM(stat_old.shape, jnp.float32), jax.ShapeDtypeStruct(stat_old.shape, jnp.float32)],
        in_specs=[SMEM] + [VMEM] * (1 + len(tiles)),
        out_specs=[VMEM, anywhere],
        scratch_shapes=[pltpu.SemaphoreType.DMA],
        compiler_params=params,
        cost_estimate=cost,
    )(place, pltpu.with_memory_space_constraint(stat_old, pltpu.VMEM), *tiles)
    layouts, tiles = with_halves([(layout, after(mine, base)) for layout, mine in tiles2])
    count = 2 * sum(len(layout) for layout in layouts)
    return pl.pallas_call(
        functools.partial(end, layouts),
        out_shape=jax.ShapeDtypeStruct(stat_old.shape, jnp.float32),
        in_specs=[SMEM] + [VMEM] * (1 + len(tiles)) + [anywhere],
        out_specs=anywhere,
        scratch_shapes=[pltpu.VMEM((count, 256, 256), jnp.float32), pltpu.SemaphoreType.DMA((count,))],
        input_output_aliases={2 + len(tiles): 0},
        compiler_params=params,
        cost_estimate=cost,
    )(place, pltpu.with_memory_space_constraint(base, pltpu.VMEM), *tiles, new)


def solution(mesh):
    placed = (P("rows", "cols"), P("cols", "rows"))
    return jax.shard_map(
        body, mesh=mesh, in_specs=placed, out_specs=P("cols", "rows"), check_vma=False
    )
```

```python
import functools

import jax
import jax.numpy as jnp
import numpy as np
from jax import lax
from jax.experimental import pallas as pl
from jax.experimental.pallas import tpu as pltpu
from jax.sharding import PartitionSpec as P


AXES = ("rows", "cols")
SIZES = (2, 4, 4, 2, 2)
ALONG = {"s": (0, 0), "a1": (1, 0), "a2": (2, 0), "a3": (3, 0), "b1": (0, 1), "b2": (0, 2), "b3": (0, 3)}
ROWS = 64.0 * 2.0 ** (np.arange(1024) * 0.6180339887 % 1 / 2)
COLUMNS = 2.0 ** (np.arange(256) * 0.7548776662 % 1 / 2)
NEAR = (
    ("a1", "s", ("right", "left"), False),
    ("a1", "a3", ("right",), False),
    ("a1", "b1", ("right", "left"), False),
)
SELF = (("s", "s", ("right",), True),)
FAR = (("b3", "a2", ("right", "left"), False),)
OPPOSITE = (("b2", "a2", ("right",), True),)
VMEM = pl.BlockSpec(memory_space=pltpu.VMEM)
SMEM = pl.BlockSpec(memory_space=pltpu.SMEM)


def offset(name, core):
    dx, dy = ALONG[name]
    return (dx, dy) if core == 0 else (-dy % 4, dx)


def gap(name, start, core):
    return tuple((a - b) % 4 for a, b in zip(offset(name, core), offset(start, core)))


def send(value, move):
    pairs = []
    for source in range(int(np.prod(SIZES))):
        place = [int(i) for i in np.unravel_index(source, SIZES)]
        pairs.append((source, int(np.ravel_multi_index(move(*place), SIZES))))
    return lax.ppermute(value, AXES, pairs)


def to_place(name, swap=False):
    def move(zh, x, y, zl, core):
        dx, dy = offset(name, core)
        if swap:
            zh, zl = zl, zh
        return zh, (x + dx) % 4, (y + dy) % 4, zl, core

    return move


def other_core(zh, x, y, zl, core):
    return zh, x, y, zl, 1 - core


def other_high(zh, x, y, zl, core):
    return 1 - zh, x, y, zl, core


def first_partner(zh, x, y, zl, core):
    return (zh, x, y, 1 - zl, core) if core == 0 else (1 - zh, x, y, 1 - zl, core)


def second_partner(zh, x, y, zl, core):
    return first_partner(zh, x, y, zl, 1 - core)[:4] + (core,)


def after(value, *others):
    return lax.optimization_barrier((value, *others))[0]


def packed(value):
    rows, columns = np.float32(ROWS[: value.shape[-2], None]), np.float32(COLUMNS)
    return (value * rows * columns).astype(jnp.float16)


def unpacked(value):
    rows, columns = np.float32(1 / ROWS[: value.shape[-2], None]), np.float32(1 / COLUMNS)
    return value.astype(jnp.float32) * rows * columns


def call(kernel, outs, place, *args, keep=True, cost=2**21):
    return pl.pallas_call(
        kernel,
        out_shape=[pltpu.VMEM(s, jnp.float32) if keep else jax.ShapeDtypeStruct(s, jnp.float32) for s in outs],
        in_specs=[SMEM] + [VMEM] * len(args),
        out_specs=[VMEM] * len(outs),
        compiler_params=pltpu.CompilerParams(vmem_limit_bytes=8 * 2**20),
        cost_estimate=pl.CostEstimate(flops=0, bytes_accessed=cost, transcendentals=0),
    )(place, *[pltpu.with_memory_space_constraint(a, pltpu.VMEM) for a in args])


def multiply(pairs, names, place, *refs):
    held = {name: refs[2 * i : 2 * i + 2] for i, name in enumerate(names)}
    out = refs[-1]
    core = place[3]
    straight = jnp.where(place[0] == place[2], 1, 0)

    def pair(left, right, halved, at):
        for kind in (0, 1):
            ends = straight if kind == 0 else 1 - straight
            lhs = held[left][kind]
            if halved and lhs.shape[0] == 256:
                lhs = lhs.at[pl.ds(pl.multiple_of(core * 128, 128), 128)]
            for col in (0, 1):
                slot = jnp.where(ends == 1, 1 if col else 2, jnp.where(core == col, 0, 3))
                out[slot, pl.ds(at, lhs.shape[0])] = lax.dot_general(
                    lhs[...], held[right][col][...], (((1,), (1,)), ((), ())), preferred_element_type=jnp.float32
                )

    at = 0
    for left, right, _, halved in pairs:
        if {left, right} & {"b1", "b3"}:
            mirror = {"b1": "b3", "b3": "b1"}
            pl.when(core == 0)(functools.partial(pair, left, right, halved, at))
            pl.when(core == 1)(functools.partial(pair, mirror.get(left, left), mirror.get(right, right), halved, at))
        else:
            pair(left, right, halved, at)
        at += 128 if halved else 256


def products(place, blocks, pairs, cost=0):
    names = {name for pair in pairs for name in pair[:2]}
    names = sorted(names | {"b1", "b3"} if names & {"b1", "b3"} else names)
    return call(
        functools.partial(multiply, pairs, names),
        [(4, sum(128 if halved else 256 for *_, halved in pairs), 256)],
        place,
        *[rows for name in names for rows in blocks[name]],
        cost=cost,
    )[0]


def finish(messages, place, *refs):
    outs = refs[-len(messages) :]
    for tiles, out in zip(messages, outs, strict=True):
        to = 0
        for size, terms in tiles:
            parts = [refs[i][pl.ds(at, size)] if slot is None else refs[i][slot, pl.ds(at, size)] for i, slot, at in terms]
            out[pl.ds(to, size)] = sum(parts[1:], parts[0])
            to += size


def delivered(place, arrays, tiles):
    messages = {}
    for (left, right, keepers, halved), terms in tiles:
        for keeper in keepers:
            to, rows = (right, left) if keeper == "right" else (left, right)
            part = (halved, [gap(rows, to, c) for c in (0, 1)], (128 if halved else 256, terms))
            messages.setdefault((to, keeper == "left"), []).append(part)
    sums = [[part[2] for part in parts] for parts in messages.values()]
    outs = call(functools.partial(finish, sums), [(sum(size for size, _ in m), 256) for m in sums], place, *arrays)
    kept = []
    for ((to, turned), parts), out in zip(messages.items(), outs, strict=True):
        if turned or to == "a2":
            out = packed(out)
        if to != "s":
            out = send(out, to_place(to, turned))
        kept.append(([(turned, halved, gaps) for halved, gaps, _ in parts], out))
    return kept, outs


def with_halves(kept):
    both = []
    for _, mine in kept:
        far = send(mine, other_core)
        both += [unpacked(part) if mine.dtype == jnp.float16 else part for part in (mine, far)]
    return [layout for layout, _ in kept], [pltpu.with_memory_space_constraint(part, pltpu.VMEM) for part in both]


def places(layouts, place, tiles):
    core = place[3]
    for parts, pair in zip(layouts, zip(tiles[::2], tiles[1::2]), strict=True):
        for source, ref in zip((core, 1 - core), pair):
            at = 0
            for turned, halved, gaps in parts:
                size = 128 if halved else 256
                dx = jnp.where(source == 0, gaps[0][0], gaps[1][0])
                dy = jnp.where(source == 0, gaps[0][1], gaps[1][1])
                x, y = (place[1] + dx) & 3, (place[4] + dy) & 3
                to = ((x & 1) * 4 + y) * 256 + (source * 128 if halved else 0)

                def tile(ref=ref, at=at, size=size, turned=turned):
                    return ref[pl.ds(at, size)].T if turned else ref[pl.ds(at, size)]

                yield (x >> 1) == core, pl.ds(pl.multiple_of(to, 128), size), tile
                at += size


def begin(layouts, place, old, *refs):
    new, out, sem = refs[-3:]
    new[...] = 0.9 * old[...]
    for ours, to, tile in places(layouts, place, refs[:-3]):

        @pl.when(ours)
        def _():
            new[to] += 0.1 * tile()

    copy = pltpu.make_async_copy(new, out, sem)
    copy.start()
    copy.wait()


def end(layouts, place, base, *refs):
    out, rows, sems = refs[-3:]
    copies = []
    for n, (ours, to, tile) in enumerate(places(layouts, place, refs[:-4])):
        size = to.size
        copy = pltpu.make_async_copy(rows.at[n, pl.ds(0, size)], out.at[to], sems.at[n])

        @pl.when(ours)
        def _():
            rows[n, pl.ds(0, size)] = base[to] + 0.1 * tile()
            copy.start()

        copies.append((ours, copy))
    for ours, copy in copies:
        pl.when(ours)(copy.wait)


def body(gradient, stat_old):
    device = lax.axis_index("rows").astype(jnp.int32)
    column = lax.axis_index("cols").astype(jnp.int32)
    zh, x, y = device >> 4, (device >> 2) & 3, device & 3
    zl, core = column >> 1, column & 1
    place = jnp.stack([zh, x, zl, core, y])
    gradient, place, zh, core = lax.optimization_barrier((gradient, place, zh, core))
    first_core = core == 0

    def whole(rows, *others):
        far = after(send(rows, other_core), *others)
        first = jnp.where(first_core, rows, far)
        return jnp.concatenate([first, jnp.where(first_core, far, rows)], axis=1)

    keep = lax.dynamic_slice_in_dim(gradient, zh * 896, 896, 1)
    give = lax.dynamic_slice_in_dim(gradient, (1 - zh) * 896, 896, 1)
    given = send(give, other_high)
    own = {"s": whole(keep)}
    own["a1"], own["a3"] = send(own["s"], to_place("a3")), send(own["s"], to_place("a1"))
    own["b1"], own["b3"] = send(own["a1"], other_core), send(own["a3"], other_core)
    other = {"s": whole(given, own["a1"], own["a3"])}
    other["a1"], other["a3"] = send(other["s"], to_place("a3")), send(other["s"], to_place("a1"))
    made0 = products(place, {"s": (own["s"], other["s"])}, SELF)
    got0 = send(packed(made0[:2]), first_partner)
    late0 = send(packed(made0[3] + unpacked(got0[1])), second_partner)
    other["a1"], other["a3"] = after((other["a1"], other["a3"]), late0)
    own["a2"] = send(after(own["a1"], other["a1"], own["b1"]), to_place("a3"))
    other["a2"] = send(after(other["a3"], own["b3"]), to_place("a1"))
    other["b1"], other["b3"] = send(other["a1"], other_core), send(other["a3"], other_core)
    blocks = {name: (own[name], other[name]) for name in own}

    made1 = products(place, blocks, NEAR, 2**24)
    leave1 = packed(made1[0]), packed(made1[1])
    got1 = send(leave1[1], first_partner)
    a2 = after(blocks["a2"], got1)
    b2 = tuple(send(jnp.where(first_core, rows[128:], rows[:128]), other_core) for rows in a2)
    pass1 = packed(made1[3] + unpacked(got1))
    late1 = send(pass1, second_partner)
    rest1 = send(after(leave1[0], pass1), first_partner)
    made2 = products(after(place, pass1), {**blocks, "a2": a2}, FAR, 2**23)
    made3 = products(place, {"a2": a2, "b2": after(b2, made2)}, OPPOSITE, 2**23)
    leave2 = packed(jnp.concatenate([made2[:2], made3[:2]], axis=1))
    got2 = send(leave2, first_partner)
    at = [256 * i for i in range(4)]
    tiles1, _ = delivered(
        place,
        [made1, unpacked(after(rest1, leave2)), unpacked(after(late1, leave2)), made0, unpacked(got0[0]), unpacked(late0)],
        [(pair, [(0, 2, at[i]), (1, None, at[i]), (2, None, at[i])]) for i, pair in enumerate(NEAR)]
        + [(SELF[0], [(3, 2, 0), (4, None, 0), (5, None, 0)])],
    )
    pass2 = packed(jnp.concatenate([made2[3], made3[3]]) + unpacked(got2[1]))
    late2 = send(pass2, second_partner)
    tiles2, _ = delivered(
        place,
        [made2, made3, unpacked(got2[0]), unpacked(after(late2, *(mine for _, mine in tiles1 if mine.dtype == jnp.float32)))],
        [
            (FAR[0], [(0, 2, 0), (2, None, 0), (3, None, 0)]),
            (OPPOSITE[0], [(1, 2, 0), (2, None, 256), (3, None, 256)]),
        ],
    )
    anywhere = pl.BlockSpec(memory_space=pl.ANY)
    params = pltpu.CompilerParams(vmem_limit_bytes=8 * 2**20)
    cost = pl.CostEstimate(flops=0, bytes_accessed=2**21, transcendentals=0)
    layouts, tiles = with_halves(tiles1)
    base, new = pl.pallas_call(
        functools.partial(begin, layouts),
        out_shape=[pltpu.VMEM(stat_old.shape, jnp.float32), jax.ShapeDtypeStruct(stat_old.shape, jnp.float32)],
        in_specs=[SMEM] + [VMEM] * (1 + len(tiles)),
        out_specs=[VMEM, anywhere],
        scratch_shapes=[pltpu.SemaphoreType.DMA],
        compiler_params=params,
        cost_estimate=cost,
    )(place, pltpu.with_memory_space_constraint(stat_old, pltpu.VMEM), *tiles)
    layouts, tiles = with_halves([(layout, after(mine, base)) for layout, mine in tiles2])
    count = 2 * sum(len(layout) for layout in layouts)
    return pl.pallas_call(
        functools.partial(end, layouts),
        out_shape=jax.ShapeDtypeStruct(stat_old.shape, jnp.float32),
        in_specs=[SMEM] + [VMEM] * (1 + len(tiles)) + [anywhere],
        out_specs=anywhere,
        scratch_shapes=[pltpu.VMEM((count, 256, 256), jnp.float32), pltpu.SemaphoreType.DMA((count,))],
        input_output_aliases={2 + len(tiles): 0},
        compiler_params=params,
        cost_estimate=cost,
    )(place, pltpu.with_memory_space_constraint(base, pltpu.VMEM), *tiles, new)


def solution(mesh):
    placed = (P("rows", "cols"), P("cols", "rows"))
    return jax.shard_map(
        body, mesh=mesh, in_specs=placed, out_specs=P("cols", "rows"), check_vma=False
    )
```

```python
import functools

import jax
import jax.numpy as jnp
import numpy as np
from jax import lax
from jax.experimental import pallas as pl
from jax.experimental.pallas import tpu as pltpu
from jax.sharding import PartitionSpec as P


AXES = ("rows", "cols")
SIZES = (2, 4, 4, 2, 2)
ALONG = {"s": (0, 0), "a1": (1, 0), "a2": (2, 0), "a3": (3, 0), "b1": (0, 1), "b2": (0, 2), "b3": (0, 3)}
ROWS = 64.0 * 2.0 ** (np.arange(1024) * 0.6180339887 % 1 / 2)
COLUMNS = 2.0 ** (np.arange(256) * 0.7548776662 % 1 / 2)
NEAR = (
    ("a1", "s", ("right", "left"), False),
    ("a1", "a3", ("right",), False),
    ("a1", "b1", ("right", "left"), False),
)
SELF = (("s", "s", ("right",), True),)
FAR = (("b3", "a2", ("right", "left"), False),)
OPPOSITE = (("b2", "a2", ("right",), True),)
VMEM = pl.BlockSpec(memory_space=pltpu.VMEM)
SMEM = pl.BlockSpec(memory_space=pltpu.SMEM)


def offset(name, core):
    dx, dy = ALONG[name]
    return (dx, dy) if core == 0 else (-dy % 4, dx)


def gap(name, start, core):
    return tuple((a - b) % 4 for a, b in zip(offset(name, core), offset(start, core)))


def send(value, move):
    pairs = []
    for source in range(int(np.prod(SIZES))):
        place = [int(i) for i in np.unravel_index(source, SIZES)]
        pairs.append((source, int(np.ravel_multi_index(move(*place), SIZES))))
    return lax.ppermute(value, AXES, pairs)


def to_place(name, swap=False):
    def move(zh, x, y, zl, core):
        dx, dy = offset(name, core)
        if swap:
            zh, zl = zl, zh
        return zh, (x + dx) % 4, (y + dy) % 4, zl, core

    return move


def other_core(zh, x, y, zl, core):
    return zh, x, y, zl, 1 - core


def other_high(zh, x, y, zl, core):
    return 1 - zh, x, y, zl, core


def first_partner(zh, x, y, zl, core):
    return (zh, x, y, 1 - zl, core) if core == 0 else (1 - zh, x, y, 1 - zl, core)


def second_partner(zh, x, y, zl, core):
    return first_partner(zh, x, y, zl, 1 - core)[:4] + (core,)


def after(value, *others):
    return lax.optimization_barrier((value, *others))[0]


def packed(value):
    rows, columns = np.float32(ROWS[: value.shape[-2], None]), np.float32(COLUMNS)
    return (value * rows * columns).astype(jnp.float16)


def unpacked(value):
    rows, columns = np.float32(1 / ROWS[: value.shape[-2], None]), np.float32(1 / COLUMNS)
    return value.astype(jnp.float32) * rows * columns


def call(kernel, outs, place, *args, keep=True, cost=2**21):
    return pl.pallas_call(
        kernel,
        out_shape=[pltpu.VMEM(s, jnp.float32) if keep else jax.ShapeDtypeStruct(s, jnp.float32) for s in outs],
        in_specs=[SMEM] + [VMEM] * len(args),
        out_specs=[VMEM] * len(outs),
        compiler_params=pltpu.CompilerParams(vmem_limit_bytes=8 * 2**20),
        cost_estimate=pl.CostEstimate(flops=0, bytes_accessed=cost, transcendentals=0),
    )(place, *[pltpu.with_memory_space_constraint(a, pltpu.VMEM) for a in args])


def multiply(pairs, names, place, *refs):
    held = {name: refs[2 * i : 2 * i + 2] for i, name in enumerate(names)}
    out = refs[-1]
    core = place[3]
    straight = jnp.where(place[0] == place[2], 1, 0)

    def pair(left, right, halved, at):
        for kind in (0, 1):
            ends = straight if kind == 0 else 1 - straight
            lhs = held[left][kind]
            if halved and lhs.shape[0] == 256:
                lhs = lhs.at[pl.ds(pl.multiple_of(core * 128, 128), 128)]
            for col in (0, 1):
                slot = jnp.where(ends == 1, 1 if col else 2, jnp.where(core == col, 0, 3))
                out[slot, pl.ds(at, lhs.shape[0])] = lax.dot_general(
                    lhs[...], held[right][col][...], (((1,), (1,)), ((), ())), preferred_element_type=jnp.float32
                )

    at = 0
    for left, right, _, halved in pairs:
        if {left, right} & {"b1", "b3"}:
            mirror = {"b1": "b3", "b3": "b1"}
            pl.when(core == 0)(functools.partial(pair, left, right, halved, at))
            pl.when(core == 1)(functools.partial(pair, mirror.get(left, left), mirror.get(right, right), halved, at))
        else:
            pair(left, right, halved, at)
        at += 128 if halved else 256


def products(place, blocks, pairs, cost=0):
    names = {name for pair in pairs for name in pair[:2]}
    names = sorted(names | {"b1", "b3"} if names & {"b1", "b3"} else names)
    return call(
        functools.partial(multiply, pairs, names),
        [(4, sum(128 if halved else 256 for *_, halved in pairs), 256)],
        place,
        *[rows for name in names for rows in blocks[name]],
        cost=cost,
    )[0]


def finish(messages, place, *refs):
    outs = refs[-len(messages) :]
    for tiles, out in zip(messages, outs, strict=True):
        to = 0
        for size, terms in tiles:
            parts = [refs[i][pl.ds(at, size)] if slot is None else refs[i][slot, pl.ds(at, size)] for i, slot, at in terms]
            out[pl.ds(to, size)] = sum(parts[1:], parts[0])
            to += size


def delivered(place, arrays, tiles):
    messages = {}
    for (left, right, keepers, halved), terms in tiles:
        for keeper in keepers:
            to, rows = (right, left) if keeper == "right" else (left, right)
            part = (halved, [gap(rows, to, c) for c in (0, 1)], (128 if halved else 256, terms))
            messages.setdefault((to, keeper == "left"), []).append(part)
    sums = [[part[2] for part in parts] for parts in messages.values()]
    outs = call(functools.partial(finish, sums), [(sum(size for size, _ in m), 256) for m in sums], place, *arrays)
    kept = []
    for ((to, turned), parts), out in zip(messages.items(), outs, strict=True):
        if turned or to == "a2":
            out = packed(out)
        if to != "s":
            out = send(out, to_place(to, turned))
        kept.append(([(turned, halved, gaps) for halved, gaps, _ in parts], out))
    return kept, outs


def with_halves(kept):
    both = []
    for _, mine in kept:
        far = send(mine, other_core)
        both += [unpacked(part) if mine.dtype == jnp.float16 else part for part in (mine, far)]
    return [layout for layout, _ in kept], [pltpu.with_memory_space_constraint(part, pltpu.VMEM) for part in both]


def places(layouts, place, tiles):
    core = place[3]
    for parts, pair in zip(layouts, zip(tiles[::2], tiles[1::2]), strict=True):
        for source, ref in zip((core, 1 - core), pair):
            at = 0
            for turned, halved, gaps in parts:
                size = 128 if halved else 256
                dx = jnp.where(source == 0, gaps[0][0], gaps[1][0])
                dy = jnp.where(source == 0, gaps[0][1], gaps[1][1])
                x, y = (place[1] + dx) & 3, (place[4] + dy) & 3
                to = ((x & 1) * 4 + y) * 256 + (source * 128 if halved else 0)

                def tile(ref=ref, at=at, size=size, turned=turned):
                    return ref[pl.ds(at, size)].T if turned else ref[pl.ds(at, size)]

                yield (x >> 1) == core, pl.ds(pl.multiple_of(to, 128), size), tile
                at += size


def begin(layouts, place, old, *refs):
    new, out, sem = refs[-3:]
    new[...] = 0.9 * old[...]
    for ours, to, tile in places(layouts, place, refs[:-3]):

        @pl.when(ours)
        def _():
            new[to] += 0.1 * tile()

    copy = pltpu.make_async_copy(new, out, sem)
    copy.start()
    copy.wait()


def end(layouts, place, base, *refs):
    out, rows, sems = refs[-3:]
    copies = []
    for n, (ours, to, tile) in enumerate(places(layouts, place, refs[:-4])):
        size = to.size
        copy = pltpu.make_async_copy(rows.at[n, pl.ds(0, size)], out.at[to], sems.at[n])

        @pl.when(ours)
        def _():
            rows[n, pl.ds(0, size)] = base[to] + 0.1 * tile()
            copy.start()

        copies.append((ours, copy))
    for ours, copy in copies:
        pl.when(ours)(copy.wait)


def body(gradient, stat_old):
    device = lax.axis_index("rows").astype(jnp.int32)
    column = lax.axis_index("cols").astype(jnp.int32)
    zh, x, y = device >> 4, (device >> 2) & 3, device & 3
    zl, core = column >> 1, column & 1
    place = jnp.stack([zh, x, zl, core, y])
    gradient, place, zh, core = lax.optimization_barrier((gradient, place, zh, core))
    first_core = core == 0

    def whole(rows, *others):
        far = after(send(rows, other_core), *others)
        first = jnp.where(first_core, rows, far)
        return jnp.concatenate([first, jnp.where(first_core, far, rows)], axis=1)

    keep = lax.dynamic_slice_in_dim(gradient, zh * 896, 896, 1)
    give = lax.dynamic_slice_in_dim(gradient, (1 - zh) * 896, 896, 1)
    given = send(give, other_high)
    own = {"s": whole(keep)}
    own["a1"], own["a3"] = send(own["s"], to_place("a3")), send(own["s"], to_place("a1"))
    own["b1"], own["b3"] = send(own["a1"], other_core), send(own["a3"], other_core)
    other = {"s": whole(given, own["a1"], own["a3"])}
    other["a1"], other["a3"] = send(other["s"], to_place("a3")), send(other["s"], to_place("a1"))
    made0 = products(place, {"s": (own["s"], other["s"])}, SELF)
    got0 = send(packed(made0[:2]), first_partner)
    late0 = send(packed(made0[3] + unpacked(got0[1])), second_partner)
    other["a1"], other["a3"] = after((other["a1"], other["a3"]), late0)
    own["a2"] = send(after(own["a1"], other["a1"], own["b1"]), to_place("a3"))
    other["a2"] = send(after(other["a3"], own["b3"]), to_place("a1"))
    other["b1"], other["b3"] = send(other["a1"], other_core), send(other["a3"], other_core)
    blocks = {name: (own[name], other[name]) for name in own}

    made1 = products(place, blocks, NEAR, 2**24)
    leave1 = packed(made1[0]), packed(made1[1])
    got1 = send(leave1[1], first_partner)
    a2 = after(blocks["a2"], got1)
    b2 = tuple(send(jnp.where(first_core, rows[128:], rows[:128]), other_core) for rows in a2)
    pass1 = packed(made1[3] + unpacked(got1))
    late1 = send(pass1, second_partner)
    rest1 = send(after(leave1[0], pass1), first_partner)
    made2 = products(after(place, pass1), {**blocks, "a2": a2}, FAR, 2**23)
    made3 = products(place, {"a2": a2, "b2": after(b2, made2)}, OPPOSITE, 2**23)
    leave2 = packed(jnp.concatenate([made2[:2], made3[:2]], axis=1))
    got2 = send(leave2, first_partner)
    at = [256 * i for i in range(4)]
    tiles1, _ = delivered(
        place,
        [made1, unpacked(after(rest1, leave2)), unpacked(after(late1, leave2)), made0, unpacked(got0[0]), unpacked(late0)],
        [(pair, [(0, 2, at[i]), (1, None, at[i]), (2, None, at[i])]) for i, pair in enumerate(NEAR)]
        + [(SELF[0], [(3, 2, 0), (4, None, 0), (5, None, 0)])],
    )
    pass2 = packed(jnp.concatenate([made2[3], made3[3]]) + unpacked(got2[1]))
    late2 = send(pass2, second_partner)
    tiles2, _ = delivered(
        place,
        [made2, made3, unpacked(got2[0]), unpacked(after(late2, *(mine for _, mine in tiles1 if mine.dtype == jnp.float32)))],
        [
            (FAR[0], [(0, 2, 0), (2, None, 0), (3, None, 0)]),
            (OPPOSITE[0], [(1, 2, 0), (2, None, 256), (3, None, 256)]),
        ],
    )
    anywhere = pl.BlockSpec(memory_space=pl.ANY)
    params = pltpu.CompilerParams(vmem_limit_bytes=8 * 2**20)
    cost = pl.CostEstimate(flops=0, bytes_accessed=2**21, transcendentals=0)
    received = [mine for _, mine in tiles1]
    layouts, tiles = with_halves([(layout, after(mine, *received)) for layout, mine in tiles1])
    base, new = pl.pallas_call(
        functools.partial(begin, layouts),
        out_shape=[pltpu.VMEM(stat_old.shape, jnp.float32), jax.ShapeDtypeStruct(stat_old.shape, jnp.float32)],
        in_specs=[SMEM] + [VMEM] * (1 + len(tiles)),
        out_specs=[VMEM, anywhere],
        scratch_shapes=[pltpu.SemaphoreType.DMA],
        compiler_params=params,
        cost_estimate=cost,
    )(place, pltpu.with_memory_space_constraint(stat_old, pltpu.VMEM), *tiles)
    layouts, tiles = with_halves([(layout, after(mine, base)) for layout, mine in tiles2])
    count = 2 * sum(len(layout) for layout in layouts)
    return pl.pallas_call(
        functools.partial(end, layouts),
        out_shape=jax.ShapeDtypeStruct(stat_old.shape, jnp.float32),
        in_specs=[SMEM] + [VMEM] * (1 + len(tiles)) + [anywhere],
        out_specs=anywhere,
        scratch_shapes=[pltpu.VMEM((count, 256, 256), jnp.float32), pltpu.SemaphoreType.DMA((count,))],
        input_output_aliases={2 + len(tiles): 0},
        compiler_params=params,
        cost_estimate=cost,
    )(place, pltpu.with_memory_space_constraint(base, pltpu.VMEM), *tiles, new)


def solution(mesh):
    placed = (P("rows", "cols"), P("cols", "rows"))
    return jax.shard_map(
        body, mesh=mesh, in_specs=placed, out_specs=P("cols", "rows"), check_vma=False
    )
```
